512 devices in a mesh: island: 16 (over y_hi, x), expert: 32 (over z, y_lo, core).
Axes of the slice: x: 4, y: 8 (y_hi: 4, y_lo: 2; y = y_hi * 2 + y_lo), z: 8, core: 2. Of those that a mesh axis runs over, the one named last changes fastest.
Arguments:
- tokens: bfloat16 [1, 65536, 5120], P(None, ('island', 'expert')), may hold values from -6 to 6
- targets: bfloat16 [1, 65536, 5120], P(None, ('island', 'expert')), may hold values from -6 to 6
- expert_ids: int32 [1, 65536, 6], P(None, ('island', 'expert')), may hold values from 0 to 159, as said below
- gate_weights: float32 [1, 65536, 6], P(None, ('island', 'expert')), may hold values from 0.1 to 1
- gate_proj: bfloat16 [3072, 5120], P('expert', 'island'), may hold values from -0.078125 to 0.078125
- up_proj: bfloat16 [3072, 5120], P('expert', 'island'), may hold values from -0.078125 to 0.078125
- down_global: float32 [3072, 5120], P('expert', 'island'), may hold values from -0.21875 to 0.21875
- outer_momentum: float32 [3072, 5120], P('expert', 'island'), may hold values from -0.003 to 0.003
- inner_first: bfloat16 [16, 3072, 5120], P('island', 'expert'), may hold values from -1.1953125 to 1.1953125
- inner_second: bfloat16 [16, 3072, 5120], P('island', 'expert'), may hold values from 0.5 to 8
Outputs:
- new_down: float32 [3072, 5120], P('expert', 'island')
- new_momentum: float32 [3072, 5120], P('expert', 'island')
The draws below stay inside these ranges and needn't reach their ends.
Inputs may be any that keep to these rules, and one draw needn't show every extreme that they name: `expert_ids`: A row's 6 ids are different. In each inner step and each aligned block of 128 rows (the rows of one device), a row names at most one id below 4, each id below 4 is named by at most 8 rows, and in every block one of them is named by exactly 8 rows.
All inputs are finite; a program needn't handle non-finite values.
Results may differ from the reference program's by a relative error of at most 0.0051.
Values may be sent and summed in bfloat16 or wider, within the bound.
A program may use at most 64 MiB of HBM per device.

```python
import math
import jax
import jax.numpy as jnp
from jax import lax

D = 5120
EXPERTS_ALL = 160
TOP = 6
FW = 768
GROUP = 8
CAP = 8
STEPS = 1
TOK_STEP = 128
H_DEV = 96
E_WIN = 4
ROWS = 65536
N_ISLAND = 16
N_EXPERT = 32


def draw_expert_ids(key, part):
    window = E_WIN
    blocks = STEPS * ROWS // TOK_STEP
    keys = jax.random.split(key, 6)
    counts = jax.random.randint(keys[0], (blocks, window), 1, CAP + 1)
    forced = jax.random.randint(keys[1], (blocks,), 0, window)
    counts = jnp.where(jnp.arange(window)[None, :] == forced[:, None], CAP, counts)
    orders = jax.vmap(lambda k: jax.random.permutation(k, TOK_STEP))(jax.random.split(keys[2], blocks))
    place = jnp.argsort(orders, axis=1)
    slot_expert = jnp.minimum(place // CAP, window - 1)
    inner = place % CAP
    limit = jnp.take_along_axis(counts, slot_expert, axis=1)
    inside = (place < window * CAP) & (inner < limit)
    stride = (EXPERTS_ALL - window) // TOP
    jumps = jax.random.randint(keys[3], (blocks, TOK_STEP, TOP), 1, stride)
    base = jax.random.randint(keys[4], (blocks, TOK_STEP, 1), 0, EXPERTS_ALL - window)
    others = window + (base + jnp.cumsum(jumps, axis=2)) % (EXPERTS_ALL - window)
    column = jax.random.randint(keys[5], (blocks, TOK_STEP, 1), 0, TOP)
    usage = inside[:, :, None] & (jnp.arange(TOP)[None, None, :] == column)
    chosen = jnp.where(usage, slot_expert[:, :, None], others)
    return chosen.reshape(STEPS, ROWS, TOP).astype(jnp.int32)


def levels(rng, dims, cuts, least, high):
    loudness, own = 1.0, jax.random.fold_in(rng, 6)
    for position, shards_of in cuts:
        draws = jnp.exp(jax.random.uniform(jax.random.fold_in(own, position), (shards_of,), jnp.float32, least / len(cuts), high / len(cuts)))
        loudness = loudness * jnp.repeat(draws, dims[position] // shards_of).reshape([-1 if axis == position else 1 for axis in range(len(dims))])
    return loudness


def noise(own_key, extent, width, most, cuts=(), held_as=jnp.bfloat16):
    factor_of = levels(own_key, extent, cuts, -0.22, 0.18) if cuts else 1.0
    drawn = jax.random.normal(own_key, extent, jnp.float32) * width * factor_of
    return jnp.minimum(jnp.maximum(drawn, -most), most).astype(held_as)


def setup_inputs(seed: int = 0) -> dict:
    seeds = jax.random.split(jax.random.key(seed), 11)
    return {
        "tokens": noise(seeds[0], (STEPS, ROWS, D), 1.0, 6.0, ((1, 512),)),
        "targets": noise(seeds[1], (STEPS, ROWS, D), 1.0, 6.0, ((1, 512),)),
        "expert_ids": draw_expert_ids(jax.random.fold_in(seeds[10], 71), 0),
        "gate_weights": jnp.clip(0.1 + 0.9 * jax.random.uniform(seeds[3], (STEPS, ROWS, TOP), jnp.float32) ** levels(seeds[3], (STEPS, ROWS, TOP), ((1, 512),), -0.2, 0.2), 0.1, 1.0),
        "gate_proj": noise(seeds[4], (E_WIN * FW, D), D ** -0.5, 0.078125, ((0, 32), (1, 16))),
        "up_proj": noise(seeds[5], (E_WIN * FW, D), D ** -0.5, 0.078125, ((0, 32), (1, 16))),
        "down_global": noise(seeds[6], (E_WIN * FW, D), FW ** -0.5, 0.21875, ((0, 32), (1, 16)), jnp.float32),
        "outer_momentum": noise(seeds[7], (E_WIN * FW, D), 0.0005, 0.003, ((0, 32), (1, 16)), jnp.float32),
        "inner_first": noise(seeds[8], (N_ISLAND, E_WIN * FW, D), 0.2, 1.1953125, ((0, 16), (1, 32))),
        "inner_second": jnp.clip(jnp.exp(math.log(8.0) - 2.7725887 * jax.random.uniform(seeds[9], (N_ISLAND, E_WIN * FW, D), jnp.float32) ** levels(seeds[9], (N_ISLAND, E_WIN * FW, D), ((0, 16), (1, 32)), -0.2, 0.2)), 0.5, 8.0).astype(jnp.bfloat16),
    }


beta_first = 0.9
beta_second = 0.95
inner_rate = 0.01
decay_rate = 0.1
epsilon = 1e-08
outer_rate = 0.7
outer_mu = 0.9

def route_table(expert_ids, gate_weights, window):
    hit = expert_ids < window
    chosen = lax.optimization_barrier(jnp.sum(jnp.where(hit, expert_ids, 0), axis=1))
    routed = jnp.any(hit, axis=1)
    weight = lax.optimization_barrier(jnp.sum(jnp.where(hit, gate_weights, jnp.zeros_like(gate_weights)), axis=1))
    member = (chosen[:, None] == jnp.arange(window, dtype=jnp.int32)[None, :]) & routed[:, None]
    rank = jnp.cumsum(member.astype(jnp.int32), axis=0) - 1
    places = member[:, :, None] & (rank[:, :, None] == jnp.arange(CAP, dtype=jnp.int32)[None, None, :])
    select = places.reshape(expert_ids.shape[0], window * CAP).T.astype(jnp.float32)
    return (select, weight)

def to_slots(values, window):
    return values.reshape(N_EXPERT, window, CAP, -1).transpose(1, 0, 2, 3).reshape(window, N_EXPERT * CAP, -1)

def reference(tokens, targets, expert_ids, gate_weights, gate_proj, up_proj, down_global, outer_momentum, inner_first, inner_second):
    window = E_WIN
    span = TOK_STEP * N_EXPERT
    gate_block = gate_proj.astype(jnp.float32).reshape(window, FW, D)
    up_block = up_proj.astype(jnp.float32).reshape(window, FW, D)

    def island(total, index):
        start = index * span
        weights = down_global
        first = lax.dynamic_index_in_dim(inner_first, index, 0, keepdims=False).astype(jnp.float32)
        second = lax.dynamic_index_in_dim(inner_second, index, 0, keepdims=False).astype(jnp.float32)
        for step in range(STEPS):
            rows = lax.dynamic_slice_in_dim(tokens[step], start, span, 0).reshape(N_EXPERT, TOK_STEP, D)
            goals = lax.dynamic_slice_in_dim(targets[step], start, span, 0).reshape(N_EXPERT, TOK_STEP, D)
            ids = lax.dynamic_slice_in_dim(expert_ids[step], start, span, 0).reshape(N_EXPERT, TOK_STEP, TOP)
            gates = lax.dynamic_slice_in_dim(gate_weights[step], start, span, 0).reshape(N_EXPERT, TOK_STEP, TOP)
            select, weight = jax.vmap(lambda a, b: route_table(a, b, window))(ids, gates)
            sent = to_slots(jnp.einsum('bst,btd->bsd', select, rows.astype(jnp.float32)), window)
            aims = to_slots(jnp.einsum('bst,btd->bsd', select, goals.astype(jnp.float32)), window)
            scales = to_slots(jnp.einsum('bst,bt->bs', select, weight, precision=lax.Precision.HIGHEST)[..., None], window)
            pre_gate = jnp.einsum('erd,efd->erf', sent, gate_block)
            pre_up = jnp.einsum('erd,efd->erf', sent, up_block)
            active = (jax.nn.silu(pre_gate) * pre_up).astype(jnp.bfloat16)
            heavy = weights.astype(jnp.bfloat16).astype(jnp.float32).reshape(window, GROUP, H_DEV, D)
            pieces = active.astype(jnp.float32).reshape(window, N_EXPERT * CAP, GROUP, H_DEV)
            parts = jnp.einsum('ergh,eghd->ergd', pieces, heavy)
            output = lax.optimization_barrier(jnp.sum(parts, axis=2))
            errors = (scales * (scales * output - aims)).astype(jnp.bfloat16)
            grads = jnp.einsum('erf,erd->efd', active.astype(jnp.float32), errors.astype(jnp.float32)).reshape(window * FW, D)
            first = beta_first * first + (1.0 - beta_first) * grads
            second = beta_second * second + (1.0 - beta_second) * grads * grads
            weights = weights - inner_rate * (first / (jnp.sqrt(second) + epsilon) + decay_rate * weights)
        return (total + (down_global - weights), None)
    total, _ = lax.scan(island, jnp.zeros(down_global.shape, jnp.float32), jnp.arange(N_ISLAND, dtype=jnp.int32))
    delta = total / N_ISLAND
    new_momentum = outer_mu * outer_momentum + delta
    new_down = down_global - outer_rate * (delta + outer_mu * new_momentum)
    return (new_down, new_momentum)
```

```python
import jax
import jax.numpy as jnp
from jax import lax
from jax.experimental import pallas as pl
from jax.experimental.pallas import tpu as pltpu
from jax.sharding import PartitionSpec as P

CAP = 8
SLOT = 2 * CAP
LANES = 128

beta_first = 0.9
beta_second = 0.95
inner_rate = 0.01
decay_rate = 0.1
epsilon = 1e-08
outer_rate = 0.7
outer_mu = 0.9

F32 = jnp.float32
BF16 = jnp.bfloat16
MESH = pl.DeviceIdType.MESH
ROWS_T = (((0,), (0,)), ((), ()))
COLS_T = (((1,), (1,)), ((), ()))


def wait_for(ref, sem):
    pltpu.make_async_copy(ref, ref, sem).wait()


def loop(low, high, body):
    lax.fori_loop(low, high, lambda i, _: (body(i), 0)[1], 0)


def kernel(
    tok_hbm, tgt_hbm, ids_ref, gw_ref, gate_ref, up_ref, down_ref, m_hbm, v_hbm,
    out_ref,
    tok, tgt, sel, sbuf, xyb, xs, xp, ys, gs, lhs,
    gut, dt, gu, dd, dx, mv, part, pr, ab, wn, eb, gr, ub, r1, st, r2,
    in_sem, gu_s, gu_r, gus1_s, d_s, d_r, ds1_s, xy_s, xy_r, xp_s, xp_r, dx_s, dx_r,
    mv_s, mv_r, p_s, p_r, a_s, a_r, u_s, u_r, t_s, t_r,
):
    isl = lax.axis_index("island")
    t = lax.axis_index("expert")
    x, yh = lax.rem(isl, 4), lax.div(isl, 4)
    e, pos = lax.div(t, 8), lax.rem(t, 8)
    c, core = lax.div(pos, 2), lax.rem(pos, 2)
    base = 8 * e
    pair = t + 1 - 2 * core
    right = yh * 4 + lax.rem(x + 1, 4)
    left = yh * 4 + lax.rem(x + 3, 4)
    hid, chunk = gate_ref.shape
    half = hid // 2
    cw = 2 * chunk
    home = c == yh
    away = c != yh

    def send(src, dst, s, r, island, expert):
        pltpu.make_async_remote_copy(
            src_ref=src, dst_ref=dst, send_sem=s, recv_sem=r,
            device_id=(island, expert), device_id_type=MESH,
        ).start()

    barrier = pltpu.get_barrier_semaphore()

    def tell(island, expert):
        pl.semaphore_signal(barrier, inc=1, device_id=(island, expert), device_id_type=MESH)

    loop(1, 32, lambda i: tell(isl, lax.rem(t + i, 32)))
    for d in range(1, 4):
        for k in range(2):
            tell(yh * 4 + lax.rem(x + d, 4), base + 2 * c + k)
        tell(lax.rem(yh + d, 4) * 4 + x, base + 2 * yh + core)

    @pl.when(away)
    def _():
        for q in range(4):
            tell(c * 4 + x, base + 2 * q + core)

    load_tok = pltpu.make_async_copy(tok_hbm, tok, in_sem.at[0])
    load_tgt = pltpu.make_async_copy(tgt_hbm, tgt, in_sem.at[1])
    load_tok.start()
    load_tgt.start()

    row = lax.broadcasted_iota(jnp.int32, (chunk, cw), 0)
    col = lax.broadcasted_iota(jnp.int32, (chunk, cw), 1)
    put0 = (col == row).astype(F32).astype(BF16)
    put1 = (col == row + chunk).astype(F32).astype(BF16)

    def dot(a, b):
        return jnp.dot(a, b, preferred_element_type=F32)

    gut[...] = (dot(gate_ref[...], put0) + dot(up_ref[...], put1)).astype(BF16)
    down = down_ref[...].astype(BF16)
    dt[...] = (dot(down[:half], put0) + dot(down[half:], put1)).astype(BF16)

    n_tok = ids_ref.shape[0]
    lane = lax.broadcasted_iota(jnp.int32, (n_tok, 4 * SLOT), 1)
    named = lax.div(lane, SLOT)
    ids = ids_ref[...]
    member = jnp.zeros((n_tok, 4 * SLOT), F32)
    for j in range(ids.shape[1]):
        member = member + (ids[:, j:j + 1] == named).astype(F32)
    before = (
        lax.broadcasted_iota(jnp.int32, (n_tok, n_tok), 1)
        < lax.broadcasted_iota(jnp.int32, (n_tok, n_tok), 0)
    ).astype(F32).astype(BF16)
    rank = dot(before, member.astype(BF16))
    picked = jnp.where(rank == lax.rem(lane, CAP).astype(F32), member, 0.0)
    of_x = lax.rem(lane, SLOT) < CAP
    same = (
        lax.broadcasted_iota(jnp.int32, (n_tok, n_tok), 1)
        == lax.broadcasted_iota(jnp.int32, (n_tok, n_tok), 0)
    ).astype(F32).astype(BF16)
    for j, part_of in enumerate((of_x, jnp.logical_not(of_x))):
        chosen = jnp.where(part_of, picked, 0.0).astype(BF16)
        sel[j] = lax.dot_general(chosen, same, ROWS_T, preferred_element_type=F32).astype(BF16)
    weight = jnp.sum(jnp.where(ids < 4, gw_ref[...], 0.0), axis=1, keepdims=True)
    high = weight.astype(BF16)
    rest = weight - high.astype(F32)
    mid = rest.astype(BF16)
    low = (rest - mid.astype(F32)).astype(BF16)
    glane = lax.broadcasted_iota(jnp.int32, (n_tok, LANES), 1)
    gmat = jnp.where(glane == 0, high.astype(F32), 0.0)
    gmat = jnp.where(glane == 1, mid.astype(F32), gmat)
    gmat = jnp.where(glane == 2, low.astype(F32), gmat)
    gates = dot(sel[0], gmat.astype(BF16)).astype(BF16)

    pl.semaphore_wait(barrier, jnp.where(away, 44, 40))

    def first_stage(tile, buf, s, r):
        for d in range(1, 4):
            send(tile, buf.at[0, c], s, r.at[0, c], lax.rem(yh + d, 4) * 4 + x, base + 2 * yh + core)

        @pl.when(away)
        def _():
            send(tile, buf.at[0, c], s, r.at[0, c], isl, base + 2 * yh + core)

        @pl.when(home)
        def _():
            pltpu.make_async_copy(tile, buf.at[0, c], r.at[0, c]).start()

    first_stage(gut, gu, gus1_s, gu_r)

    load_tok.wait()
    load_tgt.wait()

    def dispatch(p):
        cols = pl.ds(pl.multiple_of(p * cw, LANES), cw)
        sbuf[p, :, 0:cw] = (dot(sel[0], tok[:, cols]) + dot(sel[1], tgt[:, cols])).astype(BF16)
        sbuf[p, :, cw:cw + LANES] = gates
        for j in range(4):
            block = sbuf.at[p, pl.ds(j * SLOT, SLOT)]

            @pl.when(8 * j + p != t)
            def _():
                send(block, xyb.at[t], xy_s, xy_r, isl, 8 * j + p)

            @pl.when(8 * j + p == t)
            def _():
                pltpu.make_async_copy(block, xyb.at[t], xy_r).start()

    loop(0, 8, dispatch)
    first_stage(dt, dd, ds1_s, d_r)

    def moments(p):
        cols = pl.ds(pl.multiple_of(p * cw, LANES), cw)
        for j, ref in enumerate((m_hbm, v_hbm)):

            @pl.when(p != pos)
            def _():
                send(ref.at[:, cols], mv.at[j, pos], mv_s, mv_r, isl, base + p)

            @pl.when(p == pos)
            def _():
                pltpu.make_async_copy(ref.at[:, cols], mv.at[j, pos], mv_r).start()

    me = base + pos

    def around(buf, s, r):
        def body(q):
            wait_for(buf.at[0, q], r.at[0, q])
            send(buf.at[0, q], buf.at[3, q], s, r.at[3, q], right, me)
            send(buf.at[0, q], buf.at[1, q], s, r.at[1, q], left, me)

        loop(0, 4, body)

    def forward(buf, s, r):
        def body(q):
            wait_for(buf.at[3, q], r.at[3, q])
            send(buf.at[3, q], buf.at[2, q], s, r.at[2, q], right, me)
            wait_for(buf.at[1, q + 2], r.at[1, q + 2])
            send(buf.at[1, q + 2], buf.at[2, q + 2], s, r.at[2, q + 2], left, me)

        loop(0, 2, body)

    def others(buf, r):
        def body(q):
            wait_for(buf.at[3, q + 2], r.at[3, q + 2])
            wait_for(buf.at[1, q], r.at[1, q])

        loop(0, 2, body)

    def far(buf, r):
        loop(0, 4, lambda q: wait_for(buf.at[2, q], r.at[2, q]))

    around(gu, gu_s, gu_r)
    loop(0, 8, moments)

    in_low = lax.broadcasted_iota(jnp.int32, (8 * CAP, cw), 1) < chunk

    def spread(v, h, rows):
        turned = pltpu.roll(v, chunk, 1)
        up_rows = pl.ds(rows.start + 32 * CAP, rows.size)
        lhs[2 * h, rows] = jnp.where(in_low, v, 0.0).astype(BF16)
        lhs[2 * h, up_rows] = jnp.where(in_low, 0.0, turned).astype(BF16)
        lhs[2 * h + 1, rows] = jnp.where(in_low, turned, 0.0).astype(BF16)
        lhs[2 * h + 1, up_rows] = jnp.where(in_low, 0.0, v).astype(BF16)

    wait_for(xyb, xy_r)

    def unpack(i):
        v = xyb[pl.ds(8 * i, 8)].astype(F32)
        rows = pl.ds(pl.multiple_of(i * 8 * CAP, 8 * CAP), 8 * CAP)
        xv = v[:, :CAP, :cw].reshape(8 * CAP, cw)
        xs[rows] = xv.astype(BF16)
        ys[rows] = v[:, CAP:, :cw].reshape(8 * CAP, cw)
        total = jnp.sum(v[:, :CAP, cw:].reshape(8 * CAP, LANES), axis=1, keepdims=True)
        gs[rows] = jnp.broadcast_to(total, (8 * CAP, LANES))
        spread(xv, core, rows)

    loop(0, 4, unpack)
    send(xs, xp, xp_s, xp_r, isl, pair)
    forward(gu, gu_s, gu_r)
    around(dd, d_s, d_r)
    wait_for(xp, xp_r)

    def unpack_pair(i):
        rows = pl.ds(pl.multiple_of(i * 8 * CAP, 8 * CAP), 8 * CAP)
        spread(xp[rows].astype(F32), 1 - core, rows)

    loop(0, 4, unpack_pair)

    def pre(rel):
        made = lax.dot_general(
            lhs[lax.rem(x + rel, 4)], gu[rel].reshape(4 * hid, cw), COLS_T, preferred_element_type=F32
        )
        return made.reshape(2, 4, 8 * CAP, 4 * hid)

    part[...] = pre(0)
    others(gu, gu_r)
    part[...] += pre(1)
    part[...] += pre(3)
    far(gu, gu_r)
    part[...] += pre(2)
    for d in range(1, 4):
        q = lax.rem(c + d, 4)
        send(part.at[:, q], pr.at[4 - d], p_s, p_r.at[4 - d], isl, base + 2 * q + core)
    forward(dd, d_s, d_r)
    for d in range(1, 4):
        wait_for(pr.at[d], p_r.at[d])
    gate_sum = part[0, c] + pr[1, 0] + pr[2, 0] + pr[3, 0]
    up_sum = part[1, c] + pr[1, 1] + pr[2, 1] + pr[3, 1]
    mine = 4 * core + c
    ab[mine] = (gate_sum * jax.nn.sigmoid(gate_sum) * up_sum).astype(BF16)
    loop(1, 8, lambda i: send(ab.at[mine], ab.at[mine], a_s, a_r, isl, base + lax.rem(pos + i, 8)))

    others(dd, d_r)
    far(dd, d_r)
    for j in range(2):
        rel = lax.rem(2 * (1 - core) + j + 4 - x, 4)
        send(dd.at[rel], dx.at[j], dx_s, dx_r.at[j], isl, pair)
    in_low_h = lax.broadcasted_iota(jnp.int32, (half, cw), 1) < chunk

    def lay(k, q, w0, w1):
        top = pl.multiple_of(q * hid, hid)
        w0, w1 = w0.astype(F32), w1.astype(F32)
        wn[k, pl.ds(top, half)] = jnp.where(in_low_h, w0, pltpu.roll(w1, chunk, 1)).astype(BF16)
        wn[k, pl.ds(top + half, half)] = jnp.where(in_low_h, pltpu.roll(w0, chunk, 1), w1).astype(BF16)

    rel0 = lax.rem(2 * core + 4 - x, 4)
    rel1 = lax.rem(2 * core + 5 - x, 4)
    loop(0, 4, lambda q: lay(core, q, dd[rel0, q], dd[rel1, q]))
    for j in range(2):
        wait_for(dx.at[j], dx_r.at[j])
    loop(0, 4, lambda q: lay(1 - core, q, dx[0, q], dx[1, q]))

    wait_for(ab.at[pl.ds(0, 7)], a_r)

    def acts(k):
        return ab[4 * k:4 * k + 4].reshape(32 * CAP, 4 * hid)

    g = gs[:, 0:1]
    output = dot(acts(0), wn[0]) + dot(acts(1), wn[1])
    eb[...] = (g * (g * output - ys[...])).astype(BF16)
    wait_for(mv, mv_r)
    for k in range(2):
        gr[...] = lax.dot_general(acts(k), eb[...], ROWS_T, preferred_element_type=F32)

        def adam(q):
            grad = gr[pl.ds(pl.multiple_of(q * hid, hid), hid)]
            first = beta_first * mv[0, 2 * q + k].astype(F32) + (1.0 - beta_first) * grad
            second = beta_second * mv[1, 2 * q + k].astype(F32) + (1.0 - beta_second) * grad * grad
            step = first / (jnp.sqrt(second) + epsilon)
            upper, lower = step[:half], step[half:]
            ub[0, k, q] = jnp.where(in_low_h, upper, pltpu.roll(lower, chunk, 1)).astype(BF16)
            ub[1, k, q] = jnp.where(in_low_h, pltpu.roll(upper, chunk, 1), lower).astype(BF16)

        loop(0, 4, adam)
        for j in range(2):
            stays = jnp.logical_and(2 * core + j == x, core == k)

            @pl.when(jnp.logical_not(stays))
            def _():
                send(ub.at[j, k], r1.at[x], u_s.at[j, k], u_r.at[x], yh * 4 + 2 * core + j, base + 2 * c + k)

            @pl.when(stays)
            def _():
                pltpu.make_async_copy(ub.at[j, k], r1.at[x], u_r.at[x]).start()

    loop(0, 4, lambda i: wait_for(r1.at[i], u_r.at[i]))

    def column(q):
        total = r1[0, q].astype(F32) + r1[1, q].astype(F32) + r1[2, q].astype(F32) + r1[3, q].astype(F32)
        st[q] = total.astype(st.dtype)
        stays = jnp.logical_and(home, q == c)

        @pl.when(jnp.logical_not(stays))
        def _():
            send(st.at[q], r2.at[yh], t_s.at[q], t_r.at[yh], c * 4 + x, base + 2 * q + core)

        @pl.when(stays)
        def _():
            pltpu.make_async_copy(st.at[q], r2.at[yh], t_r.at[yh]).start()

    loop(0, 4, column)
    loop(0, 4, lambda i: wait_for(r2.at[i], t_r.at[i]))
    out_ref[...] = r2[0].astype(F32) + r2[1].astype(F32) + r2[2].astype(F32) + r2[3].astype(F32)

    for buf, s, s1 in ((gu, gu_s, gus1_s), (dd, d_s, ds1_s)):
        wait_for(buf.at[pl.ds(0, 3)], s)

        @pl.when(away)
        def _():
            wait_for(buf.at[0], s1)

        @pl.when(home)
        def _():
            wait_for(buf.at[0, pl.ds(0, 3)], s1)

    wait_for(xyb.at[pl.ds(0, 31)], xy_s)
    wait_for(xs, xp_s)
    wait_for(dx, dx_s)
    wait_for(mv.at[:, pl.ds(0, 7)], mv_s)
    wait_for(pr.at[pl.ds(0, 3)], p_s)
    wait_for(ab.at[pl.ds(0, 7)], a_s)
    for j in range(2):
        for k in range(2):

            @pl.when(jnp.logical_not(jnp.logical_and(2 * core + j == x, core == k)))
            def _():
                wait_for(ub.at[j, k], u_s.at[j, k])

    def left_st(q):
        @pl.when(jnp.logical_not(jnp.logical_and(home, q == c)))
        def _():
            wait_for(st.at[q], t_s.at[q])

    loop(0, 4, left_st)


def summed_steps(tokens, targets, expert_ids, gate_weights, gate_proj, up_proj, down_global, first, second):
    n_tok, width = tokens.shape
    hid, chunk = gate_proj.shape
    half, cw = hid // 2, 2 * chunk
    rows = 32 * CAP
    dma = pltpu.SemaphoreType.DMA
    anywhere = pl.BlockSpec(memory_space=pl.ANY)
    vmem = pl.BlockSpec(memory_space=pltpu.VMEM)
    scratch = [
        pltpu.VMEM((n_tok, width), BF16),
        pltpu.VMEM((n_tok, width), BF16),
        pltpu.VMEM((2, 4 * SLOT, n_tok), BF16),
        pltpu.VMEM((8, 4 * SLOT, cw + LANES), BF16),
        pltpu.VMEM((32, SLOT, cw + LANES), BF16),
        pltpu.VMEM((rows, cw), BF16),
        pltpu.VMEM((rows, cw), BF16),
        pltpu.VMEM((rows, cw), F32),
        pltpu.VMEM((rows, LANES), F32),
        pltpu.VMEM((4, 2 * rows, cw), BF16),
        pltpu.VMEM((hid, cw), BF16),
        pltpu.VMEM((half, cw), BF16),
        pltpu.VMEM((4, 4, hid, cw), BF16),
        pltpu.VMEM((4, 4, half, cw), BF16),
        pltpu.VMEM((2, 4, half, cw), BF16),
        pltpu.VMEM((2, 8, hid, cw), BF16),
        pltpu.VMEM((2, 4, 8 * CAP, 4 * hid), F32),
        pltpu.VMEM((4, 2, 8 * CAP, 4 * hid), F32),
        pltpu.VMEM((8, 8 * CAP, 4 * hid), BF16),
        pltpu.VMEM((2, 4 * hid, cw), BF16),
        pltpu.VMEM((rows, cw), BF16),
        pltpu.VMEM((4 * hid, cw), F32),
        pltpu.VMEM((2, 2, 4, half, cw), BF16),
        pltpu.VMEM((4, 4, half, cw), BF16),
        pltpu.VMEM((4, half, cw), BF16),
        pltpu.VMEM((4, half, cw), BF16),
        dma((2,)),
        dma, dma((4, 4)), dma,
        dma, dma((4, 4)), dma,
        dma, dma, dma, dma,
        dma, dma((2,)),
        dma, dma,
        dma, dma((4,)),
        dma, dma,
        dma((2, 2)), dma((4,)),
        dma((4,)), dma((4,)),
    ]
    return pl.pallas_call(
        kernel,
        out_shape=jax.ShapeDtypeStruct((half, cw), F32),
        in_specs=[anywhere, anywhere, vmem, vmem, vmem, vmem, vmem, anywhere, anywhere],
        out_specs=vmem,
        scratch_shapes=scratch,
        compiler_params=pltpu.CompilerParams(
            collective_id=0, has_side_effects=True, vmem_limit_bytes=48 * 1024 * 1024
        ),
    )(tokens, targets, expert_ids, gate_weights, gate_proj, up_proj, down_global, first, second)


def on_device(
    tokens,
    targets,
    expert_ids,
    gate_weights,
    gate_proj,
    up_proj,
    down_global,
    outer_momentum,
    inner_first,
    inner_second,
):
    islands = lax.axis_size("island")
    chunk = down_global.shape[1]
    packed = summed_steps(
        tokens[0], targets[0], expert_ids[0], gate_weights[0],
        gate_proj, up_proj, down_global, inner_first[0], inner_second[0],
    )
    total = jnp.concatenate([packed[:, :chunk], packed[:, chunk:]], axis=0)
    mean = inner_rate * (total / islands + decay_rate * down_global)
    new_momentum = outer_mu * outer_momentum + mean
    new_down = down_global - outer_rate * (mean + outer_mu * new_momentum)
    return (new_down, new_momentum)


def solution(mesh):
    return jax.shard_map(
        on_device,
        mesh=mesh,
        in_specs=(
            P(None, ("island", "expert"), None),
            P(None, ("island", "expert"), None),
            P(None, ("island", "expert"), None),
            P(None, ("island", "expert"), None),
            P("expert", "island"),
            P("expert", "island"),
            P("expert", "island"),
            P("expert", "island"),
            P("island", "expert", None),
            P("island", "expert", None),
        ),
        out_specs=(P("expert", "island"), P("expert", "island")),
        check_vma=False,
    )
```

```python
import jax
import jax.numpy as jnp
from jax import lax
from jax.experimental import pallas as pl
from jax.experimental.pallas import tpu as pltpu
from jax.sharding import PartitionSpec as P

CAP = 8
SLOT = 2 * CAP
LANES = 128

beta_first = 0.9
beta_second = 0.95
inner_rate = 0.01
decay_rate = 0.1
epsilon = 1e-08
outer_rate = 0.7
outer_mu = 0.9

F32 = jnp.float32
BF16 = jnp.bfloat16
MESH = pl.DeviceIdType.MESH
ROWS_T = (((0,), (0,)), ((), ()))
COLS_T = (((1,), (1,)), ((), ()))


def wait_for(ref, sem):
    pltpu.make_async_copy(ref, ref, sem).wait()


def loop(low, high, body):
    lax.fori_loop(low, high, lambda i, _: (body(i), 0)[1], 0)


def kernel(
    tok_hbm, tgt_hbm, ids_hbm, gw_hbm, gate_hbm, up_hbm, down_hbm, m_hbm, v_hbm,
    out_ref,
    ids_ref, gw_ref, gate_ref, up_ref, down_ref, tok, tgt, sel, sbuf, xyb, xs, xp, ys, gs, lhs,
    gut, dt, gu, dd, dx, mv, part, pb, pr, ab, wn, eb, gr, ub, r1, st, r2,
    in_sem, gu_s, gu_r, gus1_s, d_s, d_r, ds1_s, xy_s, xy_r, xp_s, xp_r, dx_s, dx_r,
    mv_s, mv_r, p_s, p_r, a_s, a_r, u_s, u_r, t_s, t_r,
):
    isl = lax.axis_index("island")
    t = lax.axis_index("expert")
    x, yh = lax.rem(isl, 4), lax.div(isl, 4)
    e, pos = lax.div(t, 8), lax.rem(t, 8)
    c, core = lax.div(pos, 2), lax.rem(pos, 2)
    base = 8 * e
    pair = t + 1 - 2 * core
    right = yh * 4 + lax.rem(x + 1, 4)
    left = yh * 4 + lax.rem(x + 3, 4)
    hid, chunk = gate_ref.shape
    half = hid // 2
    cw = 2 * chunk
    odd = lax.rem(yh, 2)

    def lag(place):
        low = 3 - 2 * place
        high = jnp.where(place == 2, 2 * odd, 2 - 2 * odd)
        return jnp.where(place < 2, low, high)

    yh_cols = lax.rem(yh + lag(c), 4)
    home = yh_cols == yh
    away = yh_cols != yh
    place_at = (2 + odd, 0, 3 - odd, 1)
    zp, yl = lax.div(c, 2), lax.rem(c, 2)

    def flip(bit, by):
        return bit + by - 2 * bit * by

    def near(i):
        return 2 * flip(zp, lax.rem(i, 2)) + flip(yl, lax.div(i, 2))

    def send(src, dst, s, r, island, expert):
        pltpu.make_async_remote_copy(
            src_ref=src, dst_ref=dst, send_sem=s, recv_sem=r,
            device_id=(island, expert), device_id_type=MESH,
        ).start()

    loads = [
        pltpu.make_async_copy(src, dst, in_sem.at[i])
        for i, (src, dst) in enumerate((
            (gate_hbm, gate_ref), (up_hbm, up_ref), (down_hbm, down_ref), (ids_hbm, ids_ref),
            (gw_hbm, gw_ref), (tok_hbm, tok), (tgt_hbm, tgt),
        ))
    ]
    for load in loads:
        load.start()

    barrier = pltpu.get_barrier_semaphore()

    def tell(island, expert):
        pl.semaphore_signal(barrier, inc=1, device_id=(island, expert), device_id_type=MESH)

    loop(1, 32, lambda i: tell(isl, lax.rem(t + i, 32)))
    for d in range(1, 4):
        for k in range(2):
            tell(yh * 4 + lax.rem(x + d, 4), base + 2 * c + k)
        tell(lax.rem(yh + d, 4) * 4 + x, base + 2 * place_at[d] + core)

    @pl.when(away)
    def _():
        for q in range(4):
            tell(yh_cols * 4 + x, base + 2 * q + core)

    for load in loads[:2]:
        load.wait()

    row = lax.broadcasted_iota(jnp.int32, (chunk, cw), 0)
    col = lax.broadcasted_iota(jnp.int32, (chunk, cw), 1)
    put0 = (col == row).astype(F32).astype(BF16)
    put1 = (col == row + chunk).astype(F32).astype(BF16)

    def dot(a, b):
        return jnp.dot(a, b, preferred_element_type=F32)

    tile = (dot(gate_ref[...], put0) + dot(up_ref[...], put1)).astype(BF16)
    gut[0] = tile[:half]
    gut[1] = tile[half:]
    pl.semaphore_wait(barrier, jnp.where(away, 44, 40))

    def first_stage(tile, at, s):
        for d in (0, 1, 3, 2):
            expert = base + 2 * place_at[d] + core
            dst, r = at
            if d:
                send(tile, dst, s, r, lax.rem(yh + d, 4) * 4 + x, expert)
            else:

                @pl.when(away)
                def _():
                    send(tile, dst, s, r, isl, expert)

                @pl.when(jnp.logical_not(away))
                def _():
                    pltpu.make_async_copy(tile, dst, r).start()

    for h in range(2):
        first_stage(gut.at[h], (gu.at[0, c, h], gu_r.at[0, c, h]), gus1_s)
    for load in loads[2:5]:
        load.wait()
    down = down_ref[...].astype(BF16)
    dt[...] = (dot(down[:half], put0) + dot(down[half:], put1)).astype(BF16)

    n_tok = tok.shape[0]
    slot = lax.broadcasted_iota(jnp.int32, (4 * SLOT, n_tok), 0)
    named = lax.div(slot, SLOT)
    member = jnp.zeros((4 * SLOT, n_tok), F32)
    weight = jnp.zeros((1, n_tok), F32)
    for j in range(ids_ref.shape[0]):
        ids = ids_ref[j]
        member = member + (ids == named).astype(F32)
        weight = weight + jnp.where(ids < 4, gw_ref[j], 0.0)
    before = (
        lax.broadcasted_iota(jnp.int32, (n_tok, n_tok), 0)
        < lax.broadcasted_iota(jnp.int32, (n_tok, n_tok), 1)
    ).astype(F32).astype(BF16)
    rank = dot(member.astype(BF16), before)
    picked = jnp.where(rank == lax.rem(slot, CAP).astype(F32), member, 0.0)
    of_x = lax.rem(slot, SLOT) < CAP
    picked_x = jnp.where(of_x, picked, 0.0)
    sel[0] = picked_x.astype(BF16)
    sel[1] = jnp.where(of_x, 0.0, picked).astype(BF16)
    value = jnp.sum(picked_x * weight, axis=1, keepdims=True)
    high = value.astype(BF16)
    rest = value - high.astype(F32)
    mid = rest.astype(BF16)
    low = (rest - mid.astype(F32)).astype(BF16)
    glane = lax.broadcasted_iota(jnp.int32, (4 * SLOT, LANES), 1)
    gates = jnp.where(glane == 0, high.astype(F32), 0.0)
    gates = jnp.where(glane == 1, mid.astype(F32), gates)
    gates = jnp.where(glane == 2, low.astype(F32), gates).astype(BF16)

    for load in loads[5:]:
        load.wait()

    def columns_of(p):
        row = lax.rem(yh + lag(lax.div(p, 2)), 4)
        return pl.ds(pl.multiple_of((2 * row + lax.rem(p, 2)) * cw, LANES), cw)

    def dispatch(p):
        cols = columns_of(p)
        sbuf[p, :, 0:cw] = (dot(sel[0], tok[:, cols]) + dot(sel[1], tgt[:, cols])).astype(BF16)
        sbuf[p, :, cw:cw + LANES] = gates
        for j in range(4):
            block = sbuf.at[p, pl.ds(j * SLOT, SLOT)]

            @pl.when(8 * j + p != t)
            def _():
                send(block, xyb.at[t], xy_s, xy_r, isl, 8 * j + p)

            @pl.when(8 * j + p == t)
            def _():
                pltpu.make_async_copy(block, xyb.at[t], xy_r).start()

    loop(0, 8, dispatch)
    first_stage(dt, (dd.at[0, c], d_r.at[0, c]), ds1_s)

    def pass_on(buf, s, r, rel, to, island, *at):
        wait_for(buf.at[(rel, *at)], r.at[(rel, *at)])
        send(buf.at[(rel, *at)], buf.at[(to, *at)], s, r.at[(to, *at)], island, t)

    def around(buf, s, r, *h):
        def body(q):
            wait_for(buf.at[(0, q, *h)], r.at[(0, q, *h)])
            for to, island in ((3, right), (1, left)):
                send(buf.at[(0, q, *h)], buf.at[(to, q, *h)], s, r.at[(to, q, *h)], island, t)

        loop(0, 4, body)

    def forward(buf, s, r, *h):
        def body(q):
            pass_on(buf, s, r, 3, 2, right, q, *h)
            pass_on(buf, s, r, 1, 2, left, q + 2, *h)

        loop(0, 2, body)

    def others(buf, r, *h):
        def body(q):
            wait_for(buf.at[(3, q + 2, *h)], r.at[(3, q + 2, *h)])
            wait_for(buf.at[(1, q, *h)], r.at[(1, q, *h)])

        loop(0, 2, body)

    def far(buf, r, *h):
        loop(0, 4, lambda q: wait_for(buf.at[(2, q, *h)], r.at[(2, q, *h)]))

    def moments(i):
        p = 2 * near(lax.div(i, 2)) + flip(core, lax.rem(i, 2))
        cols = columns_of(p)
        for j, ref in enumerate((m_hbm, v_hbm)):

            @pl.when(i > 0)
            def _():
                send(ref.at[:, cols], mv.at[i, j], mv_s, mv_r.at[i], isl, base + p)

            @pl.when(i == 0)
            def _():
                pltpu.make_async_copy(ref.at[:, cols], mv.at[i, j], mv_r.at[i]).start()

    for h in range(2):
        around(gu, gu_s, gu_r, h)
    loop(0, 8, moments)
    for h in range(2):
        forward(gu, gu_s, gu_r, h)
    around(dd, d_s, d_r)

    in_low = lax.broadcasted_iota(jnp.int32, (8 * CAP, cw), 1) < chunk

    def spread(v, h, rows):
        turned = pltpu.roll(v, chunk, 1)
        up_rows = pl.ds(rows.start + 32 * CAP, rows.size)
        lhs[2 * h, rows] = jnp.where(in_low, v, 0.0).astype(BF16)
        lhs[2 * h, up_rows] = jnp.where(in_low, 0.0, turned).astype(BF16)
        lhs[2 * h + 1, rows] = jnp.where(in_low, turned, 0.0).astype(BF16)
        lhs[2 * h + 1, up_rows] = jnp.where(in_low, 0.0, v).astype(BF16)

    wait_for(xyb, xy_r)

    def unpack(i):
        v = xyb[pl.ds(8 * i, 8)].astype(F32)
        rows = pl.ds(pl.multiple_of(i * 8 * CAP, 8 * CAP), 8 * CAP)
        xv = v[:, :CAP, :cw].reshape(8 * CAP, cw)
        xs[rows] = xv.astype(BF16)
        ys[rows] = v[:, CAP:, :cw].reshape(8 * CAP, cw)
        total = jnp.sum(v[:, :CAP, cw:].reshape(8 * CAP, LANES), axis=1, keepdims=True)
        gs[rows] = jnp.broadcast_to(total, (8 * CAP, LANES))
        spread(xv, core, rows)

    loop(0, 4, unpack)
    send(xs, xp, xp_s, xp_r, isl, pair)
    wait_for(xp, xp_r)

    def unpack_pair(i):
        rows = pl.ds(pl.multiple_of(i * 8 * CAP, 8 * CAP), 8 * CAP)
        spread(xp[rows].astype(F32), 1 - core, rows)

    loop(0, 4, unpack_pair)

    def pre(rel):
        made = lax.dot_general(
            lhs[lax.rem(x + rel, 4)], gu[rel].reshape(4 * hid, cw), COLS_T, preferred_element_type=F32
        )
        return made.reshape(2, 4, 8 * CAP, 4 * hid)

    part[...] = pre(0)
    for h in range(2):
        others(gu, gu_r, h)
    part[...] += pre(1)
    part[...] += pre(3)
    for h in range(2):
        far(gu, gu_r, h)
    part[...] += pre(2)
    pb[...] = part[...].astype(BF16)
    for d in range(1, 4):
        q = lax.rem(c + d, 4)
        send(pb.at[:, q], pr.at[4 - d], p_s, p_r.at[4 - d], isl, base + 2 * q + core)
    forward(dd, d_s, d_r)
    for d in range(1, 4):
        wait_for(pr.at[d], p_r.at[d])
    gate_sum = part[0, c] + pr[1, 0].astype(F32) + pr[2, 0].astype(F32) + pr[3, 0].astype(F32)
    up_sum = part[1, c] + pr[1, 1].astype(F32) + pr[2, 1].astype(F32) + pr[3, 1].astype(F32)
    mine = 4 * core + c
    ab[mine] = (gate_sum * jax.nn.sigmoid(gate_sum) * up_sum).astype(BF16)
    loop(1, 8, lambda i: send(ab.at[mine], ab.at[mine], a_s, a_r, isl, base + lax.rem(pos + i, 8)))

    others(dd, d_r)
    far(dd, d_r)
    for j in range(2):
        rel = lax.rem(2 * (1 - core) + j + 4 - x, 4)
        send(dd.at[rel], dx.at[j], dx_s, dx_r.at[j], isl, pair)
    in_low_h = lax.broadcasted_iota(jnp.int32, (half, cw), 1) < chunk

    def lay(k, q, w0, w1):
        top = pl.multiple_of(q * hid, hid)
        w0, w1 = w0.astype(F32), w1.astype(F32)
        wn[k, pl.ds(top, half)] = jnp.where(in_low_h, w0, pltpu.roll(w1, chunk, 1)).astype(BF16)
        wn[k, pl.ds(top + half, half)] = jnp.where(in_low_h, pltpu.roll(w0, chunk, 1), w1).astype(BF16)

    rel0 = lax.rem(2 * core + 4 - x, 4)
    rel1 = lax.rem(2 * core + 5 - x, 4)
    loop(0, 4, lambda q: lay(core, q, dd[rel0, q], dd[rel1, q]))
    for j in range(2):
        wait_for(dx.at[j], dx_r.at[j])
    loop(0, 4, lambda q: lay(1 - core, q, dx[0, q], dx[1, q]))

    wait_for(ab.at[pl.ds(0, 7)], a_r)

    def acts(k):
        return ab[4 * k:4 * k + 4].reshape(32 * CAP, 4 * hid)

    g = gs[:, 0:1]
    output = dot(acts(0), wn[0]) + dot(acts(1), wn[1])
    eb[...] = (g * (g * output - ys[...])).astype(BF16)
    for k in range(2):
        gr[k] = lax.dot_general(acts(k), eb[...], ROWS_T, preferred_element_type=F32)

    def adam(i):
        q, k = near(lax.div(i, 2)), flip(core, lax.rem(i, 2))
        grad = gr[k, pl.ds(pl.multiple_of(q * hid, hid), hid)]
        wait_for(mv.at[i], mv_r.at[i])
        first = beta_first * mv[i, 0].astype(F32) + (1.0 - beta_first) * grad
        second = beta_second * mv[i, 1].astype(F32) + (1.0 - beta_second) * grad * grad
        step = first / (jnp.sqrt(second) + epsilon)
        upper, lower = step[:half], step[half:]
        ub[i, 0] = jnp.where(in_low_h, upper, pltpu.roll(lower, chunk, 1)).astype(BF16)
        ub[i, 1] = jnp.where(in_low_h, pltpu.roll(upper, chunk, 1), lower).astype(BF16)
        for j in range(2):
            stays = jnp.logical_and(2 * core + j == x, core == k)
            dst, r = r1.at[x, q], u_r.at[x, q]

            @pl.when(jnp.logical_not(stays))
            def _():
                send(ub.at[i, j], dst, u_s, r, yh * 4 + 2 * core + j, base + 2 * c + k)

            @pl.when(stays)
            def _():
                pltpu.make_async_copy(ub.at[i, j], dst, r).start()

    loop(0, 8, adam)

    def column(i):
        q = near(i)
        for j in range(4):
            wait_for(r1.at[j, q], u_r.at[j, q])
        total = r1[0, q].astype(F32) + r1[1, q].astype(F32) + r1[2, q].astype(F32) + r1[3, q].astype(F32)
        st[q] = total.astype(st.dtype)
        stays = jnp.logical_and(home, i == 0)

        @pl.when(jnp.logical_not(stays))
        def _():
            send(st.at[q], r2.at[yh], t_s, t_r.at[yh], yh_cols * 4 + x, base + 2 * q + core)

        @pl.when(stays)
        def _():
            pltpu.make_async_copy(st.at[q], r2.at[yh], t_r.at[yh]).start()

    loop(0, 4, column)
    loop(0, 4, lambda i: wait_for(r2.at[i], t_r.at[i]))
    out_ref[...] = r2[0].astype(F32) + r2[1].astype(F32) + r2[2].astype(F32) + r2[3].astype(F32)

    for buf, s, s1 in ((gu, gu_s, gus1_s), (dd, d_s, ds1_s)):
        wait_for(buf.at[pl.ds(0, 3)], s)

        @pl.when(away)
        def _():
            wait_for(buf.at[0], s1)

        @pl.when(home)
        def _():
            wait_for(buf.at[0, pl.ds(0, 3)], s1)

    wait_for(xyb.at[pl.ds(0, 31)], xy_s)
    wait_for(xs, xp_s)
    wait_for(dx, dx_s)
    wait_for(mv.at[pl.ds(0, 7)], mv_s)
    wait_for(pr.at[pl.ds(0, 3)], p_s)
    wait_for(ab.at[pl.ds(0, 7)], a_s)
    keeps = core == lax.div(x, 2)

    @pl.when(keeps)
    def _():
        wait_for(r1.at[pl.ds(0, 3)], u_s)

    @pl.when(jnp.logical_not(keeps))
    def _():
        wait_for(r1, u_s)

    @pl.when(home)
    def _():
        wait_for(st.at[pl.ds(0, 3)], t_s)

    @pl.when(away)
    def _():
        wait_for(st, t_s)


def summed_steps(tokens, targets, expert_ids, gate_weights, gate_proj, up_proj, down_global, first, second):
    n_tok, width = tokens.shape
    hid, chunk = gate_proj.shape
    half, cw = hid // 2, 2 * chunk
    rows = 32 * CAP
    dma = pltpu.SemaphoreType.DMA
    hbm = pl.BlockSpec(memory_space=pltpu.HBM)
    vmem = pl.BlockSpec(memory_space=pltpu.VMEM)
    scratch = [
        pltpu.VMEM(expert_ids.shape, jnp.int32),
        pltpu.VMEM(gate_weights.shape, F32),
        pltpu.VMEM((hid, chunk), BF16),
        pltpu.VMEM((hid, chunk), BF16),
        pltpu.VMEM((hid, chunk), F32),
        pltpu.VMEM((n_tok, width), BF16),
        pltpu.VMEM((n_tok, width), BF16),
        pltpu.VMEM((2, 4 * SLOT, n_tok), BF16),
        pltpu.VMEM((8, 4 * SLOT, cw + LANES), BF16),
        pltpu.VMEM((32, SLOT, cw + LANES), BF16),
        pltpu.VMEM((rows, cw), BF16),
        pltpu.VMEM((rows, cw), BF16),
        pltpu.VMEM((rows, cw), F32),
        pltpu.VMEM((rows, LANES), F32),
        pltpu.VMEM((4, 2 * rows, cw), BF16),
        pltpu.VMEM((2, half, cw), BF16),
        pltpu.VMEM((half, cw), BF16),
        pltpu.VMEM((4, 4, 2, half, cw), BF16),
        pltpu.VMEM((4, 4, half, cw), BF16),
        pltpu.VMEM((2, 4, half, cw), BF16),
        pltpu.VMEM((8, 2, hid, cw), BF16),
        pltpu.VMEM((2, 4, 8 * CAP, 4 * hid), F32),
        pltpu.VMEM((2, 4, 8 * CAP, 4 * hid), BF16),
        pltpu.VMEM((4, 2, 8 * CAP, 4 * hid), BF16),
        pltpu.VMEM((8, 8 * CAP, 4 * hid), BF16),
        pltpu.VMEM((2, 4 * hid, cw), BF16),
        pltpu.VMEM((rows, cw), BF16),
        pltpu.VMEM((2, 4 * hid, cw), F32),
        pltpu.VMEM((8, 2, half, cw), BF16),
        pltpu.VMEM((4, 4, half, cw), BF16),
        pltpu.VMEM((4, half, cw), BF16),
        pltpu.VMEM((4, half, cw), BF16),
        dma((7,)),
        dma, dma((4, 4, 2)), dma,
        dma, dma((4, 4)), dma,
        dma, dma, dma, dma,
        dma, dma((2,)),
        dma, dma((8,)),
        dma, dma((4,)),
        dma, dma,
        dma, dma((4, 4)),
        dma, dma((4,)),
    ]
    return pl.pallas_call(
        kernel,
        out_shape=jax.ShapeDtypeStruct((half, cw), F32),
        in_specs=[hbm] * 9,
        out_specs=vmem,
        scratch_shapes=scratch,
        compiler_params=pltpu.CompilerParams(
            collective_id=0, has_side_effects=True, vmem_limit_bytes=64 * 1024 * 1024
        ),
    )(tokens, targets, expert_ids, gate_weights, gate_proj, up_proj, down_global, first, second)


def on_device(
    tokens,
    targets,
    expert_ids,
    gate_weights,
    gate_proj,
    up_proj,
    down_global,
    outer_momentum,
    inner_first,
    inner_second,
):
    islands = lax.axis_size("island")
    chunk = down_global.shape[1]
    packed = summed_steps(
        tokens[0], targets[0],
        jnp.transpose(expert_ids, (2, 0, 1)), jnp.transpose(gate_weights, (2, 0, 1)),
        gate_proj, up_proj, down_global, inner_first[0], inner_second[0],
    )
    total = jnp.concatenate([packed[:, :chunk], packed[:, chunk:]], axis=0)
    mean = inner_rate * (total / islands + decay_rate * down_global)
    new_momentum = outer_mu * outer_momentum + mean
    new_down = down_global - outer_rate * (mean + outer_mu * new_momentum)
    return (new_down, new_momentum)


def solution(mesh):
    return jax.shard_map(
        on_device,
        mesh=mesh,
        in_specs=(
            P(None, ("island", "expert"), None),
            P(None, ("island", "expert"), None),
            P(None, ("island", "expert"), None),
            P(None, ("island", "expert"), None),
            P("expert", "island"),
            P("expert", "island"),
            P("expert", "island"),
            P("expert", "island"),
            P("island", "expert", None),
            P("island", "expert", None),
        ),
        out_specs=(P("expert", "island"), P("expert", "island")),
        check_vma=False,
    )
```

```python
import jax
import jax.numpy as jnp
from jax import lax
from jax.experimental import pallas as pl
from jax.experimental.pallas import tpu as pltpu
from jax.sharding import PartitionSpec as P

CAP = 8
SLOT = 2 * CAP
LANES = 128

beta_first = 0.9
beta_second = 0.95
inner_rate = 0.01
decay_rate = 0.1
epsilon = 1e-08
outer_rate = 0.7
outer_mu = 0.9

F32 = jnp.float32
BF16 = jnp.bfloat16
MESH = pl.DeviceIdType.MESH
ROWS_T = (((0,), (0,)), ((), ()))
COLS_T = (((1,), (1,)), ((), ()))


def wait_for(ref, sem):
    pltpu.make_async_copy(ref, ref, sem).wait()


def loop(low, high, body):
    lax.fori_loop(low, high, lambda i, _: (body(i), 0)[1], 0)


def kernel(
    tok_hbm, tgt_hbm, ids_hbm, gw_hbm, gate_hbm, up_hbm, down_hbm, m_hbm, v_hbm,
    out_ref,
    ids_ref, gw_ref, gate_ref, up_ref, down_ref, tok, tgt, sel, grow, gbuf, sbuf, xyb, xs, xp, ys, gs, lhs,
    gut, dt, gu, dd, dx, mv, part, pb, pr, ab, wn, eb, own, gr, ub, r1, st, r2,
    in_sem, gu_s, gu_r, gus1_s, d_s, d_r, ds1_s, xy_s, xy_r, g_s, g_r, xp_s, xp_r, dx_s, dx_r,
    mv_s, mv_r, p_s, p_r, a_s, a_r, e_s, e_r, u_s, u_r, t_s, t_r,
):
    isl = lax.axis_index("island")
    t = lax.axis_index("expert")
    x, yh = lax.rem(isl, 4), lax.div(isl, 4)
    e, pos = lax.div(t, 8), lax.rem(t, 8)
    c, core = lax.div(pos, 2), lax.rem(pos, 2)
    base = 8 * e
    pair = t + 1 - 2 * core
    right = yh * 4 + lax.rem(x + 1, 4)
    left = yh * 4 + lax.rem(x + 3, 4)
    hid, chunk = gate_ref.shape
    half = hid // 2
    cw = 2 * chunk
    odd = lax.rem(yh, 2)

    def lag(place):
        low = 3 - 2 * place
        high = jnp.where(place == 2, 2 * odd, 2 - 2 * odd)
        return jnp.where(place < 2, low, high)

    yh_cols = lax.rem(yh + lag(c), 4)
    home = yh_cols == yh
    away = yh_cols != yh
    place_at = (2 + odd, 0, 3 - odd, 1)
    zp, yl = lax.div(c, 2), lax.rem(c, 2)

    def flip(bit, by):
        return bit + by - 2 * bit * by

    def beside(dz, dy):
        return 2 * flip(zp, dz) + flip(yl, dy)

    def near(i):
        return beside(lax.rem(i, 2), lax.div(i, 2))

    def send(src, dst, s, r, island, expert):
        pltpu.make_async_remote_copy(
            src_ref=src, dst_ref=dst, send_sem=s, recv_sem=r,
            device_id=(island, expert), device_id_type=MESH,
        ).start()

    loads = [
        pltpu.make_async_copy(src, dst, in_sem.at[i])
        for i, (src, dst) in enumerate((
            (gate_hbm, gate_ref), (up_hbm, up_ref), (down_hbm, down_ref), (ids_hbm, ids_ref),
            (gw_hbm, gw_ref), (tok_hbm, tok), (tgt_hbm, tgt),
        ))
    ]
    for load in loads:
        load.start()

    barrier = pltpu.get_barrier_semaphore()

    def tell(island, expert):
        pl.semaphore_signal(barrier, inc=1, device_id=(island, expert), device_id_type=MESH)

    loop(1, 32, lambda i: tell(isl, lax.rem(t + i, 32)))
    for d in range(1, 4):
        for k in range(2):
            tell(yh * 4 + lax.rem(x + d, 4), base + 2 * c + k)
        tell(lax.rem(yh + d, 4) * 4 + x, base + 2 * place_at[d] + core)
        tell(lax.rem(yh + d, 4) * 4 + x, t)

    @pl.when(away)
    def _():
        for q in range(4):
            tell(yh_cols * 4 + x, base + 2 * q + core)

    for load in loads[:2]:
        load.wait()

    row = lax.broadcasted_iota(jnp.int32, (chunk, cw), 0)
    col = lax.broadcasted_iota(jnp.int32, (chunk, cw), 1)
    put0 = (col == row).astype(F32).astype(BF16)
    put1 = (col == row + chunk).astype(F32).astype(BF16)

    def dot(a, b):
        return jnp.dot(a, b, preferred_element_type=F32)

    tile = (dot(gate_ref[...], put0) + dot(up_ref[...], put1)).astype(BF16)
    gut[0] = tile[:half]
    gut[1] = tile[half:]
    pl.semaphore_wait(barrier, jnp.where(away, 47, 43))

    def first_stage(tile, at, s):
        for d in (0, 1, 3, 2):
            expert = base + 2 * place_at[d] + core
            dst, r = at
            if d:
                send(tile, dst, s, r, lax.rem(yh + d, 4) * 4 + x, expert)
            else:

                @pl.when(away)
                def _():
                    send(tile, dst, s, r, isl, expert)

                @pl.when(jnp.logical_not(away))
                def _():
                    pltpu.make_async_copy(tile, dst, r).start()

    for h in range(2):
        first_stage(gut.at[h], (gu.at[0, c, h], gu_r.at[0, c, h]), gus1_s)
    for load in loads[2:5]:
        load.wait()
    down = down_ref[...].astype(BF16)
    dt[...] = (dot(down[:half], put0) + dot(down[half:], put1)).astype(BF16)

    n_tok = tok.shape[0]
    slot = lax.broadcasted_iota(jnp.int32, (4 * SLOT, n_tok), 0)
    named = lax.div(slot, SLOT)
    member = jnp.zeros((4 * SLOT, n_tok), F32)
    weight = jnp.zeros((1, n_tok), F32)
    for j in range(ids_ref.shape[0]):
        ids = ids_ref[j]
        member = member + (ids == named).astype(F32)
        weight = weight + jnp.where(ids < 4, gw_ref[j], 0.0)
    before = (
        lax.broadcasted_iota(jnp.int32, (n_tok, n_tok), 0)
        < lax.broadcasted_iota(jnp.int32, (n_tok, n_tok), 1)
    ).astype(F32).astype(BF16)
    rank = dot(member.astype(BF16), before)
    picked = jnp.where(rank == lax.rem(slot, CAP).astype(F32), member, 0.0)
    of_x = lax.rem(slot, SLOT) < CAP
    picked_x = jnp.where(of_x, picked, 0.0)
    sel[0] = picked_x.astype(BF16)
    sel[1] = jnp.where(of_x, 0.0, picked).astype(BF16)
    high = weight.astype(BF16)
    rest = weight - high.astype(F32)
    mid = rest.astype(BF16)
    low = (rest - mid.astype(F32)).astype(BF16)
    layer = lax.broadcasted_iota(jnp.int32, (8, n_tok), 0)
    three = jnp.where(layer == 0, high.astype(F32), 0.0)
    three = jnp.where(layer == 1, mid.astype(F32), three)
    three = jnp.where(layer == 2, low.astype(F32), three).astype(BF16)
    split = lax.dot_general(three, sel[0], COLS_T, preferred_element_type=F32)
    grow[...] = jnp.zeros(grow.shape, F32)
    grow[:, 0:4 * SLOT] = split[0:1] + split[1:2] + split[2:3]

    for load in loads[5:]:
        load.wait()

    def columns_of(p):
        row = lax.rem(yh + lag(lax.div(p, 2)), 4)
        return pl.ds(pl.multiple_of((2 * row + lax.rem(p, 2)) * cw, LANES), cw)

    def dispatch(p):
        cols = columns_of(p)
        sbuf[p] = (dot(sel[0], tok[:, cols]) + dot(sel[1], tgt[:, cols])).astype(BF16)
        for j in range(4):
            block = sbuf.at[p, pl.ds(j * SLOT, SLOT)]

            @pl.when(8 * j + p != t)
            def _():
                send(block, xyb.at[t], xy_s, xy_r, isl, 8 * j + p)
                send(grow, gbuf.at[t], g_s, g_r, isl, 8 * j + p)

            @pl.when(8 * j + p == t)
            def _():
                pltpu.make_async_copy(block, xyb.at[t], xy_r).start()
                pltpu.make_async_copy(grow, gbuf.at[t], g_r).start()

    loop(0, 8, dispatch)
    first_stage(dt, (dd.at[0, c], d_r.at[0, c]), ds1_s)

    def pass_on(buf, s, r, rel, to, island, *at):
        wait_for(buf.at[(rel, *at)], r.at[(rel, *at)])
        send(buf.at[(rel, *at)], buf.at[(to, *at)], s, r.at[(to, *at)], island, t)

    def around(buf, s, r, *h):
        def body(q):
            wait_for(buf.at[(0, q, *h)], r.at[(0, q, *h)])
            for to, island in ((3, right), (1, left)):
                send(buf.at[(0, q, *h)], buf.at[(to, q, *h)], s, r.at[(to, q, *h)], island, t)

        loop(0, 4, body)

    def forward(buf, s, r, *h):
        def body(q):
            pass_on(buf, s, r, 3, 2, right, q, *h)
            pass_on(buf, s, r, 1, 2, left, q + 2, *h)

        loop(0, 2, body)

    def others(buf, r, *h):
        def body(q):
            wait_for(buf.at[(3, q + 2, *h)], r.at[(3, q + 2, *h)])
            wait_for(buf.at[(1, q, *h)], r.at[(1, q, *h)])

        loop(0, 2, body)

    def far(buf, r, *h):
        loop(0, 4, lambda q: wait_for(buf.at[(2, q, *h)], r.at[(2, q, *h)]))

    def moments(i):
        here, there = columns_of(2 * near(i) + core), columns_of(2 * near(i) + 1 - core)
        for j, ref in enumerate((m_hbm, v_hbm)):
            pltpu.make_async_copy(ref.at[:, here], mv.at[i, 0, j], mv_r.at[0]).start()
            send(ref.at[:, there], mv.at[i, 1, j], mv_s, mv_r.at[1], isl, pair)

    for h in range(2):
        around(gu, gu_s, gu_r, h)
    loop(0, 4, moments)
    for h in range(2):
        forward(gu, gu_s, gu_r, h)
    around(dd, d_s, d_r)

    in_low = lax.broadcasted_iota(jnp.int32, (8 * CAP, cw), 1) < chunk

    def spread(v, h, rows):
        turned = pltpu.roll(v, chunk, 1)
        up_rows = pl.ds(rows.start + 32 * CAP, rows.size)
        lhs[2 * h, rows] = jnp.where(in_low, v, 0.0).astype(BF16)
        lhs[2 * h, up_rows] = jnp.where(in_low, 0.0, turned).astype(BF16)
        lhs[2 * h + 1, rows] = jnp.where(in_low, turned, 0.0).astype(BF16)
        lhs[2 * h + 1, up_rows] = jnp.where(in_low, 0.0, v).astype(BF16)

    wait_for(xyb, xy_r)
    wait_for(gbuf, g_r)

    is_own = lax.broadcasted_iota(jnp.int32, (8 * CAP, LANES), 1) == SLOT * e + lax.rem(
        lax.broadcasted_iota(jnp.int32, (8 * CAP, LANES), 0), CAP
    )

    def unpack(i):
        v = xyb[pl.ds(8 * i, 8)].astype(F32)
        rows = pl.ds(pl.multiple_of(i * 8 * CAP, 8 * CAP), 8 * CAP)
        xv = v[:, :CAP].reshape(8 * CAP, cw)
        xs[rows] = xv.astype(BF16)
        ys[rows] = v[:, CAP:].reshape(8 * CAP, cw)
        every = jnp.broadcast_to(gbuf[pl.ds(8 * i, 8)], (8, CAP, LANES)).reshape(8 * CAP, LANES)
        total = jnp.sum(jnp.where(is_own, every, 0.0), axis=1, keepdims=True)
        gs[rows] = jnp.broadcast_to(total, (8 * CAP, LANES))
        spread(xv, core, rows)

    loop(0, 4, unpack)
    send(xs, xp, xp_s, xp_r, isl, pair)
    wait_for(xp, xp_r)

    def unpack_pair(i):
        rows = pl.ds(pl.multiple_of(i * 8 * CAP, 8 * CAP), 8 * CAP)
        spread(xp[rows].astype(F32), 1 - core, rows)

    loop(0, 4, unpack_pair)

    def pre(rel):
        made = lax.dot_general(
            lhs[lax.rem(x + rel, 4)], gu[rel].reshape(4 * hid, cw), COLS_T, preferred_element_type=F32
        )
        return made.reshape(2, 4, 8 * CAP, 4 * hid)

    part[...] = pre(0)
    for h in range(2):
        others(gu, gu_r, h)
    part[...] += pre(1)
    part[...] += pre(3)
    for h in range(2):
        far(gu, gu_r, h)
    part[...] += pre(2)
    pb[...] = part[...].astype(BF16)
    for d in range(1, 4):
        q = lax.rem(c + d, 4)
        send(pb.at[:, q], pr.at[4 - d], p_s, p_r.at[4 - d], isl, base + 2 * q + core)
    forward(dd, d_s, d_r)
    for d in range(1, 4):
        wait_for(pr.at[d], p_r.at[d])
    gate_sum = part[0, c] + pr[1, 0].astype(F32) + pr[2, 0].astype(F32) + pr[3, 0].astype(F32)
    up_sum = part[1, c] + pr[1, 1].astype(F32) + pr[2, 1].astype(F32) + pr[3, 1].astype(F32)
    mine = 4 * core + c
    ab[mine] = (gate_sum * jax.nn.sigmoid(gate_sum) * up_sum).astype(BF16)
    loop(1, 8, lambda i: send(ab.at[mine], ab.at[mine], a_s, a_r, isl, base + lax.rem(pos + i, 8)))

    others(dd, d_r)
    far(dd, d_r)
    for j in range(2):
        rel = lax.rem(2 * (1 - core) + j + 4 - x, 4)
        send(dd.at[rel], dx.at[j], dx_s, dx_r.at[j], isl, pair)
    in_low_h = lax.broadcasted_iota(jnp.int32, (half, cw), 1) < chunk

    def lay(k, q, w0, w1):
        top = pl.multiple_of(q * hid, hid)
        w0, w1 = w0.astype(F32), w1.astype(F32)
        wn[k, pl.ds(top, half)] = jnp.where(in_low_h, w0, pltpu.roll(w1, chunk, 1)).astype(BF16)
        wn[k, pl.ds(top + half, half)] = jnp.where(in_low_h, pltpu.roll(w0, chunk, 1), w1).astype(BF16)

    rel0 = lax.rem(2 * core + 4 - x, 4)
    rel1 = lax.rem(2 * core + 5 - x, 4)
    loop(0, 4, lambda q: lay(core, q, dd[rel0, q], dd[rel1, q]))
    for j in range(2):
        wait_for(dx.at[j], dx_r.at[j])
    loop(0, 4, lambda q: lay(1 - core, q, dx[0, q], dx[1, q]))

    wait_for(ab.at[pl.ds(0, 7)], a_r)

    def acts(k):
        return ab[4 * k:4 * k + 4].reshape(32 * CAP, 4 * hid)

    g = gs[:, 0:1]
    output = dot(acts(0), wn[0]) + dot(acts(1), wn[1])
    eb[0] = (g * (g * output - ys[...])).astype(BF16)
    for i, (dz, dy) in ((1, (1, 0)), (2, (0, 1)), (3, (1, 1))):
        send(eb.at[0], eb.at[i], e_s, e_r.at[i], isl, base + 2 * beside(dz, dy) + core)

    unit = lax.broadcasted_iota(jnp.int32, (4 * hid, 2 * hid), 0)
    place = lax.broadcasted_iota(jnp.int32, (4 * hid, 2 * hid), 1)
    of_core = lax.div(place, hid)
    want = c * hid + lax.rem(place, hid)
    taken = [
        dot(acts(k), jnp.logical_and(unit == want, of_core == k).astype(F32).astype(BF16)) for k in range(2)
    ]
    own[...] = (taken[0] + taken[1]).astype(BF16)
    for j in range(2):
        wait_for(mv.at[pl.ds(0, 2)], mv_r.at[j])

    def step_of(i):
        @pl.when(i > 0)
        def _():
            wait_for(eb.at[i], e_r.at[i])

        gr[...] = lax.dot_general(own[...], eb[i], ROWS_T, preferred_element_type=F32)
        for k in range(2):
            grad = gr[k * hid:(k + 1) * hid]
            side = flip(core, k)
            first = beta_first * mv[i, side, 0].astype(F32) + (1.0 - beta_first) * grad
            second = beta_second * mv[i, side, 1].astype(F32) + (1.0 - beta_second) * grad * grad
            step = first / (jnp.sqrt(second) + epsilon)
            upper, lower = step[:half], step[half:]
            ub[i, k, 0] = jnp.where(in_low_h, upper, pltpu.roll(lower, chunk, 1)).astype(BF16)
            ub[i, k, 1] = jnp.where(in_low_h, pltpu.roll(upper, chunk, 1), lower).astype(BF16)
            for j in range(2):
                stays = jnp.logical_and(2 * core + j == x, core == k)
                dst, r = r1.at[x, i], u_r.at[x, i]

                @pl.when(jnp.logical_not(stays))
                def _():
                    send(ub.at[i, k, j], dst, u_s, r, yh * 4 + 2 * core + j, base + 2 * c + k)

                @pl.when(stays)
                def _():
                    pltpu.make_async_copy(ub.at[i, k, j], dst, r).start()

    def column(i):
        for j in range(4):
            wait_for(r1.at[j, i], u_r.at[j, i])
        total = r1[0, i].astype(F32) + r1[1, i].astype(F32) + r1[2, i].astype(F32) + r1[3, i].astype(F32)
        st[i] = total.astype(st.dtype)
        to = lax.rem(yh + lag(near(i)), 4)

        @pl.when(to != yh)
        def _():
            send(st.at[i], r2.at[yh], t_s, t_r.at[yh], to * 4 + x, t)

        @pl.when(to == yh)
        def _():
            pltpu.make_async_copy(st.at[i], r2.at[yh], t_r.at[yh]).start()

    def both(i):
        step_of(i)

        @pl.when(i > 0)
        def _():
            column(i - 1)

    loop(0, 4, both)
    column(jnp.int32(3))
    loop(0, 4, lambda i: wait_for(r2.at[i], t_r.at[i]))
    out_ref[...] = r2[0].astype(F32) + r2[1].astype(F32) + r2[2].astype(F32) + r2[3].astype(F32)

    for buf, s, s1 in ((gu, gu_s, gus1_s), (dd, d_s, ds1_s)):
        wait_for(buf.at[pl.ds(0, 3)], s)

        @pl.when(away)
        def _():
            wait_for(buf.at[0], s1)

        @pl.when(home)
        def _():
            wait_for(buf.at[0, pl.ds(0, 3)], s1)

    wait_for(xyb.at[pl.ds(0, 31)], xy_s)
    wait_for(gbuf.at[pl.ds(0, 31)], g_s)
    wait_for(eb.at[pl.ds(0, 3)], e_s)
    wait_for(xs, xp_s)
    wait_for(dx, dx_s)
    wait_for(mv.at[pl.ds(0, 2)], mv_s)
    wait_for(pr.at[pl.ds(0, 3)], p_s)
    wait_for(ab.at[pl.ds(0, 7)], a_s)
    keeps = core == lax.div(x, 2)

    @pl.when(keeps)
    def _():
        wait_for(r1.at[pl.ds(0, 3)], u_s)

    @pl.when(jnp.logical_not(keeps))
    def _():
        wait_for(r1, u_s)

    wait_for(st.at[pl.ds(0, 3)], t_s)


def summed_steps(tokens, targets, expert_ids, gate_weights, gate_proj, up_proj, down_global, first, second):
    n_tok, width = tokens.shape
    hid, chunk = gate_proj.shape
    half, cw = hid // 2, 2 * chunk
    rows = 32 * CAP
    dma = pltpu.SemaphoreType.DMA
    hbm = pl.BlockSpec(memory_space=pltpu.HBM)
    vmem = pl.BlockSpec(memory_space=pltpu.VMEM)
    scratch = [
        pltpu.VMEM(expert_ids.shape, jnp.int32),
        pltpu.VMEM(gate_weights.shape, F32),
        pltpu.VMEM((hid, chunk), BF16),
        pltpu.VMEM((hid, chunk), BF16),
        pltpu.VMEM((hid, chunk), F32),
        pltpu.VMEM((n_tok, width), BF16),
        pltpu.VMEM((n_tok, width), BF16),
        pltpu.VMEM((2, 4 * SLOT, n_tok), BF16),
        pltpu.VMEM((1, LANES), F32),
        pltpu.VMEM((32, 1, LANES), F32),
        pltpu.VMEM((8, 4 * SLOT, cw), BF16),
        pltpu.VMEM((32, SLOT, cw), BF16),
        pltpu.VMEM((rows, cw), BF16),
        pltpu.VMEM((rows, cw), BF16),
        pltpu.VMEM((rows, cw), F32),
        pltpu.VMEM((rows, LANES), F32),
        pltpu.VMEM((4, 2 * rows, cw), BF16),
        pltpu.VMEM((2, half, cw), BF16),
        pltpu.VMEM((half, cw), BF16),
        pltpu.VMEM((4, 4, 2, half, cw), BF16),
        pltpu.VMEM((4, 4, half, cw), BF16),
        pltpu.VMEM((2, 4, half, cw), BF16),
        pltpu.VMEM((4, 2, 2, hid, cw), BF16),
        pltpu.VMEM((2, 4, 8 * CAP, 4 * hid), F32),
        pltpu.VMEM((2, 4, 8 * CAP, 4 * hid), BF16),
        pltpu.VMEM((4, 2, 8 * CAP, 4 * hid), BF16),
        pltpu.VMEM((8, 8 * CAP, 4 * hid), BF16),
        pltpu.VMEM((2, 4 * hid, cw), BF16),
        pltpu.VMEM((4, rows, cw), BF16),
        pltpu.VMEM((rows, 2 * hid), BF16),
        pltpu.VMEM((2 * hid, cw), F32),
        pltpu.VMEM((4, 2, 2, half, cw), BF16),
        pltpu.VMEM((4, 4, half, cw), BF16),
        pltpu.VMEM((4, half, cw), BF16),
        pltpu.VMEM((4, half, cw), BF16),
        dma((7,)),
        dma, dma((4, 4, 2)), dma,
        dma, dma((4, 4)), dma,
        dma, dma, dma, dma, dma, dma,
        dma, dma((2,)),
        dma, dma((2,)),
        dma, dma((4,)),
        dma, dma,
        dma, dma((4,)),
        dma, dma((4, 4)),
        dma, dma((4,)),
    ]
    return pl.pallas_call(
        kernel,
        out_shape=jax.ShapeDtypeStruct((half, cw), F32),
        in_specs=[hbm] * 9,
        out_specs=vmem,
        scratch_shapes=scratch,
        compiler_params=pltpu.CompilerParams(
            collective_id=0, has_side_effects=True, vmem_limit_bytes=64 * 1024 * 1024
        ),
    )(tokens, targets, expert_ids, gate_weights, gate_proj, up_proj, down_global, first, second)


def on_device(
    tokens,
    targets,
    expert_ids,
    gate_weights,
    gate_proj,
    up_proj,
    down_global,
    outer_momentum,
    inner_first,
    inner_second,
):
    islands = lax.axis_size("island")
    chunk = down_global.shape[1]
    packed = summed_steps(
        tokens[0], targets[0],
        jnp.transpose(expert_ids, (2, 0, 1)), jnp.transpose(gate_weights, (2, 0, 1)),
        gate_proj, up_proj, down_global, inner_first[0], inner_second[0],
    )
    total = jnp.concatenate([packed[:, :chunk], packed[:, chunk:]], axis=0)
    mean = inner_rate * (total / islands + decay_rate * down_global)
    new_momentum = outer_mu * outer_momentum + mean
    new_down = down_global - outer_rate * (mean + outer_mu * new_momentum)
    return (new_down, new_momentum)


def solution(mesh):
    return jax.shard_map(
        on_device,
        mesh=mesh,
        in_specs=(
            P(None, ("island", "expert"), None),
            P(None, ("island", "expert"), None),
            P(None, ("island", "expert"), None),
            P(None, ("island", "expert"), None),
            P("expert", "island"),
            P("expert", "island"),
            P("expert", "island"),
            P("expert", "island"),
            P("island", "expert", None),
            P("island", "expert", None),
        ),
        out_specs=(P("expert", "island"), P("expert", "island")),
        check_vma=False,
    )
```

```python
import jax
import jax.numpy as jnp
from jax import lax
from jax.experimental import pallas as pl
from jax.experimental.pallas import tpu as pltpu
from jax.sharding import PartitionSpec as P

CAP = 8
SLOT = 2 * CAP
LANES = 128

beta_first = 0.9
beta_second = 0.95
inner_rate = 0.01
decay_rate = 0.1
epsilon = 1e-08
outer_rate = 0.7
outer_mu = 0.9

F32 = jnp.float32
BF16 = jnp.bfloat16
MESH = pl.DeviceIdType.MESH
ROWS_T = (((0,), (0,)), ((), ()))
COLS_T = (((1,), (1,)), ((), ()))


def wait_for(ref, sem):
    pltpu.make_async_copy(ref, ref, sem).wait()


def loop(low, high, body):
    lax.fori_loop(low, high, lambda i, _: (body(i), 0)[1], 0)


def kernel(
    tok_hbm, tgt_hbm, ids_hbm, gw_hbm, gate_hbm, up_hbm, down_hbm, m_hbm, v_hbm,
    out_ref,
    ids_ref, gw_ref, gate_ref, up_ref, down_ref, tok, tgt, sel, grow, gbuf, sbuf, xyb, xs, xp, ys, gs, lhs,
    gut, dt, gu, dd, dx, mv, part, pb, pr, ab, wn, eb, own, gr, ub, r1, st, r2,
    in_sem, gu_s, gu_r, gus1_s, d_s, d_r, ds1_s, xy_s, xy_r, g_s, g_r, xp_s, xp_r, dx_s, dx_r,
    mv_s, mv_r, p_s, p_r, a_s, a_r, e_s, e_r, u_s, u_r, t_s, t_r,
):
    isl = lax.axis_index("island")
    t = lax.axis_index("expert")
    x, yh = lax.rem(isl, 4), lax.div(isl, 4)
    e, pos = lax.div(t, 8), lax.rem(t, 8)
    c, core = lax.div(pos, 2), lax.rem(pos, 2)
    base = 8 * e
    pair = t + 1 - 2 * core
    right = yh * 4 + lax.rem(x + 1, 4)
    left = yh * 4 + lax.rem(x + 3, 4)
    hid, chunk = gate_ref.shape
    half = hid // 2
    cw = 2 * chunk
    odd = lax.rem(yh, 2)

    def lag(place):
        low = 3 - 2 * place
        high = jnp.where(place == 2, 2 * odd, 2 - 2 * odd)
        return jnp.where(place < 2, low, high)

    yh_cols = lax.rem(yh + lag(c), 4)
    home = yh_cols == yh
    away = yh_cols != yh
    place_at = (2 + odd, 0, 3 - odd, 1)
    zp, yl = lax.div(c, 2), lax.rem(c, 2)

    def flip(bit, by):
        return bit + by - 2 * bit * by

    def beside(dz, dy):
        return 2 * flip(zp, dz) + flip(yl, dy)

    diagonal = beside(1, 1)

    def chip(i):
        return beside(jnp.where(i == 2, 1, 0), jnp.where(i == 3, 1, 0))

    def send(src, dst, s, r, island, expert):
        pltpu.make_async_remote_copy(
            src_ref=src, dst_ref=dst, send_sem=s, recv_sem=r,
            device_id=(island, expert), device_id_type=MESH,
        ).start()

    loads = [
        pltpu.make_async_copy(src, dst, in_sem.at[i])
        for i, (src, dst) in enumerate((
            (gate_hbm, gate_ref), (up_hbm, up_ref), (down_hbm, down_ref), (ids_hbm, ids_ref),
            (gw_hbm, gw_ref), (tok_hbm, tok), (tgt_hbm, tgt),
        ))
    ]
    for load in loads:
        load.start()

    barrier = pltpu.get_barrier_semaphore()

    def tell(island, expert):
        pl.semaphore_signal(barrier, inc=1, device_id=(island, expert), device_id_type=MESH)

    loop(1, 32, lambda i: tell(isl, lax.rem(t + i, 32)))
    for d in range(1, 4):
        for k in range(2):
            tell(yh * 4 + lax.rem(x + d, 4), base + 2 * c + k)
        tell(lax.rem(yh + d, 4) * 4 + x, base + 2 * place_at[d] + core)
        tell(lax.rem(yh + d, 4) * 4 + x, t)

    @pl.when(away)
    def _():
        for q in range(4):
            tell(yh_cols * 4 + x, base + 2 * q + core)

    for load in loads[:2]:
        load.wait()

    row = lax.broadcasted_iota(jnp.int32, (chunk, cw), 0)
    col = lax.broadcasted_iota(jnp.int32, (chunk, cw), 1)
    put0 = (col == row).astype(F32).astype(BF16)
    put1 = (col == row + chunk).astype(F32).astype(BF16)

    def dot(a, b):
        return jnp.dot(a, b, preferred_element_type=F32)

    tile = (dot(gate_ref[...], put0) + dot(up_ref[...], put1)).astype(BF16)
    gut[0] = tile[:half]
    gut[1] = tile[half:]
    pl.semaphore_wait(barrier, jnp.where(away, 47, 43))

    def first_stage(tile, at, s):
        for d in (0, 1, 3, 2):
            expert = base + 2 * place_at[d] + core
            dst, r = at
            if d:
                send(tile, dst, s, r, lax.rem(yh + d, 4) * 4 + x, expert)
            else:

                @pl.when(away)
                def _():
                    send(tile, dst, s, r, isl, expert)

                @pl.when(jnp.logical_not(away))
                def _():
                    pltpu.make_async_copy(tile, dst, r).start()

    for h in range(2):
        first_stage(gut.at[h], (gu.at[0, c, h], gu_r.at[0, c, h]), gus1_s)
    for load in loads[2:5]:
        load.wait()
    down = down_ref[...].astype(BF16)
    dt[...] = (dot(down[:half], put0) + dot(down[half:], put1)).astype(BF16)

    n_tok = tok.shape[0]
    slot = lax.broadcasted_iota(jnp.int32, (4 * SLOT, n_tok), 0)
    named = lax.div(slot, SLOT)
    member = jnp.zeros((4 * SLOT, n_tok), F32)
    weight = jnp.zeros((1, n_tok), F32)
    for j in range(ids_ref.shape[0]):
        ids = ids_ref[j]
        member = member + (ids == named).astype(F32)
        weight = weight + jnp.where(ids < 4, gw_ref[j], 0.0)
    before = (
        lax.broadcasted_iota(jnp.int32, (n_tok, n_tok), 0)
        < lax.broadcasted_iota(jnp.int32, (n_tok, n_tok), 1)
    ).astype(F32).astype(BF16)
    rank = dot(member.astype(BF16), before)
    picked = jnp.where(rank == lax.rem(slot, CAP).astype(F32), member, 0.0)
    of_x = lax.rem(slot, SLOT) < CAP
    picked_x = jnp.where(of_x, picked, 0.0)
    sel[0] = picked_x.astype(BF16)
    sel[1] = jnp.where(of_x, 0.0, picked).astype(BF16)
    high = weight.astype(BF16)
    rest = weight - high.astype(F32)
    mid = rest.astype(BF16)
    low = (rest - mid.astype(F32)).astype(BF16)
    layer = lax.broadcasted_iota(jnp.int32, (8, n_tok), 0)
    three = jnp.where(layer == 0, high.astype(F32), 0.0)
    three = jnp.where(layer == 1, mid.astype(F32), three)
    three = jnp.where(layer == 2, low.astype(F32), three).astype(BF16)
    split = lax.dot_general(three, sel[0], COLS_T, preferred_element_type=F32)
    grow[...] = jnp.zeros(grow.shape, F32)
    grow[:, 0:4 * SLOT] = split[0:1] + split[1:2] + split[2:3]

    for load in loads[5:]:
        load.wait()

    def columns_of(p):
        row = lax.rem(yh + lag(lax.div(p, 2)), 4)
        return pl.ds(pl.multiple_of((2 * row + lax.rem(p, 2)) * cw, LANES), cw)

    def dispatch(p):
        cols = columns_of(p)
        sbuf[p] = (dot(sel[0], tok[:, cols]) + dot(sel[1], tgt[:, cols])).astype(BF16)
        for j in range(4):
            block = sbuf.at[p, pl.ds(j * SLOT, SLOT)]

            @pl.when(8 * j + p != t)
            def _():
                send(block, xyb.at[t], xy_s, xy_r, isl, 8 * j + p)
                send(grow, gbuf.at[t], g_s, g_r, isl, 8 * j + p)

            @pl.when(8 * j + p == t)
            def _():
                pltpu.make_async_copy(block, xyb.at[t], xy_r).start()
                pltpu.make_async_copy(grow, gbuf.at[t], g_r).start()

    loop(0, 8, dispatch)
    first_stage(dt, (dd.at[0, c], d_r.at[0, c]), ds1_s)

    def pass_on(buf, s, r, rel, to, island, *at):
        wait_for(buf.at[(rel, *at)], r.at[(rel, *at)])
        send(buf.at[(rel, *at)], buf.at[(to, *at)], s, r.at[(to, *at)], island, t)

    def around(buf, s, r, *h):
        def body(q):
            wait_for(buf.at[(0, q, *h)], r.at[(0, q, *h)])
            for to, island in ((3, right), (1, left)):
                send(buf.at[(0, q, *h)], buf.at[(to, q, *h)], s, r.at[(to, q, *h)], island, t)

        loop(0, 4, body)

    def forward(buf, s, r, *h):
        def body(q):
            pass_on(buf, s, r, 3, 2, right, q, *h)
            pass_on(buf, s, r, 1, 2, left, q + 2, *h)

        loop(0, 2, body)

    def others(buf, r, *h):
        def body(q):
            wait_for(buf.at[(3, q + 2, *h)], r.at[(3, q + 2, *h)])
            wait_for(buf.at[(1, q, *h)], r.at[(1, q, *h)])

        loop(0, 2, body)

    def far(buf, r, *h):
        loop(0, 4, lambda q: wait_for(buf.at[(2, q, *h)], r.at[(2, q, *h)]))

    def moments(n):
        i = n + jnp.where(n > 0, 1, 0)
        here, there = columns_of(2 * chip(i) + core), columns_of(2 * chip(i) + 1 - core)
        for j, ref in enumerate((m_hbm, v_hbm)):
            pltpu.make_async_copy(ref.at[:, here], mv.at[i, 0, j], mv_r.at[0]).start()
            send(ref.at[:, there], mv.at[i, 1, j], mv_s.at[0], mv_r.at[1], isl, pair)

    def moments_across(k):
        other = flip(core, k)
        cols = columns_of(2 * diagonal + other)
        for j, ref in enumerate((m_hbm, v_hbm)):
            send(ref.at[:, cols], mv.at[1, k, j], mv_s.at[1], mv_r.at[2 + k], isl, base + 2 * diagonal + other)

    for h in range(2):
        around(gu, gu_s, gu_r, h)
    loop(0, 3, moments)
    loop(0, 2, moments_across)
    for h in range(2):
        forward(gu, gu_s, gu_r, h)
    around(dd, d_s, d_r)

    in_low = lax.broadcasted_iota(jnp.int32, (8 * CAP, cw), 1) < chunk

    def spread(v, h, rows):
        turned = pltpu.roll(v, chunk, 1)
        up_rows = pl.ds(rows.start + 32 * CAP, rows.size)
        lhs[2 * h, rows] = jnp.where(in_low, v, 0.0).astype(BF16)
        lhs[2 * h, up_rows] = jnp.where(in_low, 0.0, turned).astype(BF16)
        lhs[2 * h + 1, rows] = jnp.where(in_low, turned, 0.0).astype(BF16)
        lhs[2 * h + 1, up_rows] = jnp.where(in_low, 0.0, v).astype(BF16)

    wait_for(xyb, xy_r)
    wait_for(gbuf, g_r)

    is_own = lax.broadcasted_iota(jnp.int32, (8 * CAP, LANES), 1) == SLOT * e + lax.rem(
        lax.broadcasted_iota(jnp.int32, (8 * CAP, LANES), 0), CAP
    )

    def unpack(i):
        v = xyb[pl.ds(8 * i, 8)].astype(F32)
        rows = pl.ds(pl.multiple_of(i * 8 * CAP, 8 * CAP), 8 * CAP)
        xv = v[:, :CAP].reshape(8 * CAP, cw)
        xs[rows] = xv.astype(BF16)
        ys[rows] = v[:, CAP:].reshape(8 * CAP, cw)
        every = jnp.broadcast_to(gbuf[pl.ds(8 * i, 8)], (8, CAP, LANES)).reshape(8 * CAP, LANES)
        total = jnp.sum(jnp.where(is_own, every, 0.0), axis=1, keepdims=True)
        gs[rows] = jnp.broadcast_to(total, (8 * CAP, LANES))
        spread(xv, core, rows)

    loop(0, 4, unpack)
    send(xs, xp, xp_s, xp_r, isl, pair)
    wait_for(xp, xp_r)

    def unpack_pair(i):
        rows = pl.ds(pl.multiple_of(i * 8 * CAP, 8 * CAP), 8 * CAP)
        spread(xp[rows].astype(F32), 1 - core, rows)

    loop(0, 4, unpack_pair)

    def pre(rel):
        made = lax.dot_general(
            lhs[lax.rem(x + rel, 4)], gu[rel].reshape(4 * hid, cw), COLS_T, preferred_element_type=F32
        )
        return made.reshape(2, 4, 8 * CAP, 4 * hid)

    part[...] = pre(0)
    for h in range(2):
        others(gu, gu_r, h)
    part[...] += pre(1)
    part[...] += pre(3)
    for h in range(2):
        far(gu, gu_r, h)
    part[...] += pre(2)
    pb[...] = part[...].astype(BF16)
    for d in range(1, 4):
        q = lax.rem(c + d, 4)
        send(pb.at[:, q], pr.at[4 - d], p_s, p_r.at[4 - d], isl, base + 2 * q + core)
    forward(dd, d_s, d_r)
    for d in range(1, 4):
        wait_for(pr.at[d], p_r.at[d])
    gate_sum = part[0, c] + pr[1, 0].astype(F32) + pr[2, 0].astype(F32) + pr[3, 0].astype(F32)
    up_sum = part[1, c] + pr[1, 1].astype(F32) + pr[2, 1].astype(F32) + pr[3, 1].astype(F32)
    mine = 4 * core + c
    ab[mine] = (gate_sum * jax.nn.sigmoid(gate_sum) * up_sum).astype(BF16)
    loop(1, 8, lambda i: send(ab.at[mine], ab.at[mine], a_s, a_r, isl, base + lax.rem(pos + i, 8)))

    others(dd, d_r)
    far(dd, d_r)
    for j in range(2):
        rel = lax.rem(2 * (1 - core) + j + 4 - x, 4)
        send(dd.at[rel], dx.at[j], dx_s, dx_r.at[j], isl, pair)
    in_low_h = lax.broadcasted_iota(jnp.int32, (half, cw), 1) < chunk

    def lay(k, q, w0, w1):
        top = pl.multiple_of(q * hid, hid)
        w0, w1 = w0.astype(F32), w1.astype(F32)
        wn[k, pl.ds(top, half)] = jnp.where(in_low_h, w0, pltpu.roll(w1, chunk, 1)).astype(BF16)
        wn[k, pl.ds(top + half, half)] = jnp.where(in_low_h, pltpu.roll(w0, chunk, 1), w1).astype(BF16)

    rel0 = lax.rem(2 * core + 4 - x, 4)
    rel1 = lax.rem(2 * core + 5 - x, 4)
    loop(0, 4, lambda q: lay(core, q, dd[rel0, q], dd[rel1, q]))
    for j in range(2):
        wait_for(dx.at[j], dx_r.at[j])
    loop(0, 4, lambda q: lay(1 - core, q, dx[0, q], dx[1, q]))

    wait_for(ab.at[pl.ds(0, 7)], a_r)

    def acts(k):
        return ab[4 * k:4 * k + 4].reshape(32 * CAP, 4 * hid)

    g = gs[:, 0:1]
    output = dot(acts(0), wn[0]) + dot(acts(1), wn[1])
    eb[0] = (g * (g * output - ys[...])).astype(BF16)
    for i, to in ((1, beside(1, 0)), (2, beside(0, 1))):
        send(eb.at[0], eb.at[i], e_s, e_r.at[i], isl, base + 2 * to + core)

    unit = lax.broadcasted_iota(jnp.int32, (4 * hid, 2 * hid), 0)
    place = lax.broadcasted_iota(jnp.int32, (4 * hid, 2 * hid), 1)
    of_core = lax.div(place, hid)
    for i, at in ((0, c), (1, diagonal)):
        want = at * hid + lax.rem(place, hid)
        taken = [
            dot(acts(k), jnp.logical_and(unit == want, of_core == k).astype(F32).astype(BF16))
            for k in range(2)
        ]
        own[i] = (taken[0] + taken[1]).astype(BF16)
    wait_for(mv.at[pl.ds(0, 3), 0], mv_r.at[0])
    wait_for(mv.at[pl.ds(0, 3), 0], mv_r.at[1])
    for k in range(2):
        wait_for(mv.at[1, k], mv_r.at[2 + k])

    def step_of(i):
        errors = jnp.maximum(i - 1, 0)

        @pl.when(i > 1)
        def _():
            wait_for(eb.at[errors], e_r.at[errors])

        gr[...] = lax.dot_general(own[jnp.where(i == 1, 1, 0)], eb[errors], ROWS_T, preferred_element_type=F32)
        for k in range(2):
            grad = gr[k * hid:(k + 1) * hid]
            side = flip(core, k)
            first = beta_first * mv[i, side, 0].astype(F32) + (1.0 - beta_first) * grad
            second = beta_second * mv[i, side, 1].astype(F32) + (1.0 - beta_second) * grad * grad
            step = first / (jnp.sqrt(second) + epsilon)
            upper, lower = step[:half], step[half:]
            ub[i, k, 0] = jnp.where(in_low_h, upper, pltpu.roll(lower, chunk, 1)).astype(BF16)
            ub[i, k, 1] = jnp.where(in_low_h, pltpu.roll(upper, chunk, 1), lower).astype(BF16)
            for j in range(2):
                stays = jnp.logical_and(2 * core + j == x, core == k)
                dst, r = r1.at[x, i], u_r.at[x, i]

                @pl.when(jnp.logical_not(stays))
                def _():
                    send(ub.at[i, k, j], dst, u_s, r, yh * 4 + 2 * core + j, base + 2 * c + k)

                @pl.when(stays)
                def _():
                    pltpu.make_async_copy(ub.at[i, k, j], dst, r).start()

    def column(i):
        for j in range(4):
            wait_for(r1.at[j, i], u_r.at[j, i])
        total = r1[0, i].astype(F32) + r1[1, i].astype(F32) + r1[2, i].astype(F32) + r1[3, i].astype(F32)
        st[i] = total.astype(st.dtype)
        to = lax.rem(yh + lag(chip(i)), 4)
        stays = jnp.logical_and(to == yh, i != 1)

        @pl.when(jnp.logical_not(stays))
        def _():
            expert = jnp.where(i == 1, base + 2 * diagonal + core, t)
            send(st.at[i], r2.at[yh], t_s, t_r.at[yh], to * 4 + x, expert)

        @pl.when(stays)
        def _():
            pltpu.make_async_copy(st.at[i], r2.at[yh], t_r.at[yh]).start()

    def both(i):
        step_of(i)

        @pl.when(i > 0)
        def _():
            column(i - 1)

    loop(0, 4, both)
    column(jnp.int32(3))
    loop(0, 4, lambda i: wait_for(r2.at[i], t_r.at[i]))
    out_ref[...] = r2[0].astype(F32) + r2[1].astype(F32) + r2[2].astype(F32) + r2[3].astype(F32)

    for buf, s, s1 in ((gu, gu_s, gus1_s), (dd, d_s, ds1_s)):
        wait_for(buf.at[pl.ds(0, 3)], s)

        @pl.when(away)
        def _():
            wait_for(buf.at[0], s1)

        @pl.when(home)
        def _():
            wait_for(buf.at[0, pl.ds(0, 3)], s1)

    wait_for(xyb.at[pl.ds(0, 31)], xy_s)
    wait_for(gbuf.at[pl.ds(0, 31)], g_s)
    wait_for(eb.at[pl.ds(0, 2)], e_s)
    wait_for(xs, xp_s)
    wait_for(dx, dx_s)
    wait_for(mv.at[pl.ds(0, 3), 0], mv_s.at[0])
    wait_for(mv.at[0], mv_s.at[1])
    wait_for(pr.at[pl.ds(0, 3)], p_s)
    wait_for(ab.at[pl.ds(0, 7)], a_s)
    keeps = core == lax.div(x, 2)

    @pl.when(keeps)
    def _():
        wait_for(r1.at[pl.ds(0, 3)], u_s)

    @pl.when(jnp.logical_not(keeps))
    def _():
        wait_for(r1, u_s)

    @pl.when(lag(diagonal) == 0)
    def _():
        wait_for(st, t_s)

    @pl.when(lag(diagonal) != 0)
    def _():
        wait_for(st.at[pl.ds(0, 3)], t_s)


def summed_steps(tokens, targets, expert_ids, gate_weights, gate_proj, up_proj, down_global, first, second):
    n_tok, width = tokens.shape
    hid, chunk = gate_proj.shape
    half, cw = hid // 2, 2 * chunk
    rows = 32 * CAP
    dma = pltpu.SemaphoreType.DMA
    hbm = pl.BlockSpec(memory_space=pltpu.HBM)
    vmem = pl.BlockSpec(memory_space=pltpu.VMEM)
    scratch = [
        pltpu.VMEM(expert_ids.shape, jnp.int32),
        pltpu.VMEM(gate_weights.shape, F32),
        pltpu.VMEM((hid, chunk), BF16),
        pltpu.VMEM((hid, chunk), BF16),
        pltpu.VMEM((hid, chunk), F32),
        pltpu.VMEM((n_tok, width), BF16),
        pltpu.VMEM((n_tok, width), BF16),
        pltpu.VMEM((2, 4 * SLOT, n_tok), BF16),
        pltpu.VMEM((1, LANES), F32),
        pltpu.VMEM((32, 1, LANES), F32),
        pltpu.VMEM((8, 4 * SLOT, cw), BF16),
        pltpu.VMEM((32, SLOT, cw), BF16),
        pltpu.VMEM((rows, cw), BF16),
        pltpu.VMEM((rows, cw), BF16),
        pltpu.VMEM((rows, cw), F32),
        pltpu.VMEM((rows, LANES), F32),
        pltpu.VMEM((4, 2 * rows, cw), BF16),
        pltpu.VMEM((2, half, cw), BF16),
        pltpu.VMEM((half, cw), BF16),
        pltpu.VMEM((4, 4, 2, half, cw), BF16),
        pltpu.VMEM((4, 4, half, cw), BF16),
        pltpu.VMEM((2, 4, half, cw), BF16),
        pltpu.VMEM((4, 2, 2, hid, cw), BF16),
        pltpu.VMEM((2, 4, 8 * CAP, 4 * hid), F32),
        pltpu.VMEM((2, 4, 8 * CAP, 4 * hid), BF16),
        pltpu.VMEM((4, 2, 8 * CAP, 4 * hid), BF16),
        pltpu.VMEM((8, 8 * CAP, 4 * hid), BF16),
        pltpu.VMEM((2, 4 * hid, cw), BF16),
        pltpu.VMEM((3, rows, cw), BF16),
        pltpu.VMEM((2, rows, 2 * hid), BF16),
        pltpu.VMEM((2 * hid, cw), F32),
        pltpu.VMEM((4, 2, 2, half, cw), BF16),
        pltpu.VMEM((4, 4, half, cw), BF16),
        pltpu.VMEM((4, half, cw), BF16),
        pltpu.VMEM((4, half, cw), BF16),
        dma((7,)),
        dma, dma((4, 4, 2)), dma,
        dma, dma((4, 4)), dma,
        dma, dma, dma, dma, dma, dma,
        dma, dma((2,)),
        dma((2,)), dma((4,)),
        dma, dma((4,)),
        dma, dma,
        dma, dma((3,)),
        dma, dma((4, 4)),
        dma, dma((4,)),
    ]
    return pl.pallas_call(
        kernel,
        out_shape=jax.ShapeDtypeStruct((half, cw), F32),
        in_specs=[hbm] * 9,
        out_specs=vmem,
        scratch_shapes=scratch,
        compiler_params=pltpu.CompilerParams(
            collective_id=0, has_side_effects=True, vmem_limit_bytes=64 * 1024 * 1024
        ),
    )(tokens, targets, expert_ids, gate_weights, gate_proj, up_proj, down_global, first, second)


def on_device(
    tokens,
    targets,
    expert_ids,
    gate_weights,
    gate_proj,
    up_proj,
    down_global,
    outer_momentum,
    inner_first,
    inner_second,
):
    islands = lax.axis_size("island")
    chunk = down_global.shape[1]
    packed = summed_steps(
        tokens[0], targets[0],
        jnp.transpose(expert_ids, (2, 0, 1)), jnp.transpose(gate_weights, (2, 0, 1)),
        gate_proj, up_proj, down_global, inner_first[0], inner_second[0],
    )
    total = jnp.concatenate([packed[:, :chunk], packed[:, chunk:]], axis=0)
    mean = inner_rate * (total / islands + decay_rate * down_global)
    new_momentum = outer_mu * outer_momentum + mean
    new_down = down_global - outer_rate * (mean + outer_mu * new_momentum)
    return (new_down, new_momentum)


def solution(mesh):
    return jax.shard_map(
        on_device,
        mesh=mesh,
        in_specs=(
            P(None, ("island", "expert"), None),
            P(None, ("island", "expert"), None),
            P(None, ("island", "expert"), None),
            P(None, ("island", "expert"), None),
            P("expert", "island"),
            P("expert", "island"),
            P("expert", "island"),
            P("expert", "island"),
            P("island", "expert", None),
            P("island", "expert", None),
        ),
        out_specs=(P("expert", "island"), P("expert", "island")),
        check_vma=False,
    )
```

```python
import jax
import jax.numpy as jnp
from jax import lax
from jax.experimental import pallas as pl
from jax.experimental.pallas import tpu as pltpu
from jax.sharding import PartitionSpec as P

CAP = 8
SLOT = 2 * CAP
LANES = 128

beta_first = 0.9
beta_second = 0.95
inner_rate = 0.01
decay_rate = 0.1
epsilon = 1e-08
outer_rate = 0.7
outer_mu = 0.9

F32 = jnp.float32
BF16 = jnp.bfloat16
MESH = pl.DeviceIdType.MESH
ROWS_T = (((0,), (0,)), ((), ()))
COLS_T = (((1,), (1,)), ((), ()))


def wait_for(ref, sem):
    pltpu.make_async_copy(ref, ref, sem).wait()


def loop(low, high, body):
    lax.fori_loop(low, high, lambda i, _: (body(i), 0)[1], 0)


def kernel(
    tok_hbm, tgt_hbm, ids_hbm, gw_hbm, gate_hbm, up_hbm, down_hbm, m_hbm, v_hbm,
    out_ref,
    ids_ref, gw_ref, gate_ref, up_ref, down_ref, tok, tgt, sel, grow, gbuf, sbuf, xyb, xs, xp, ys, gs, lhs,
    gut, dt, gu, dd, dx, mv, part, pb, pr, ab, wn, eb, own, gr, ub, r1, st, r2,
    in_sem, gu_s, gu_r, gus1_s, d_s, d_r, ds1_s, xy_s, xy_r, g_s, g_r, xp_s, xp_r, dx_s, dx_r,
    mv_s, mv_r, p_s, p_r, a_s, a_r, e_s, e_r, u_s, u_r, t_s, t_r,
):
    isl = lax.axis_index("island")
    t = lax.axis_index("expert")
    x, yh = lax.rem(isl, 4), lax.div(isl, 4)
    e, pos = lax.div(t, 8), lax.rem(t, 8)
    c, core = lax.div(pos, 2), lax.rem(pos, 2)
    base = 8 * e
    pair = t + 1 - 2 * core
    right = yh * 4 + lax.rem(x + 1, 4)
    left = yh * 4 + lax.rem(x + 3, 4)
    hid, chunk = gate_ref.shape
    half = hid // 2
    cw = 2 * chunk
    odd = lax.rem(yh, 2)

    def lag(place):
        low = 3 - 2 * place
        high = jnp.where(place == 2, 2 * odd, 2 - 2 * odd)
        return jnp.where(place < 2, low, high)

    yh_cols = lax.rem(yh + lag(c), 4)
    home = yh_cols == yh
    away = yh_cols != yh
    place_at = (2 + odd, 0, 3 - odd, 1)
    zp, yl = lax.div(c, 2), lax.rem(c, 2)

    def flip(bit, by):
        return bit + by - 2 * bit * by

    def beside(dz, dy):
        return 2 * flip(zp, dz) + flip(yl, dy)

    def near(i):
        return beside(lax.rem(i, 2), lax.div(i, 2))

    def send(src, dst, s, r, island, expert):
        pltpu.make_async_remote_copy(
            src_ref=src, dst_ref=dst, send_sem=s, recv_sem=r,
            device_id=(island, expert), device_id_type=MESH,
        ).start()

    loads = [
        pltpu.make_async_copy(src, dst, in_sem.at[i])
        for i, (src, dst) in enumerate((
            (gate_hbm, gate_ref), (up_hbm, up_ref), (down_hbm, down_ref), (ids_hbm, ids_ref),
            (gw_hbm, gw_ref), (tok_hbm, tok), (tgt_hbm, tgt),
        ))
    ]
    for load in loads:
        load.start()

    barrier = pltpu.get_barrier_semaphore()

    def tell(island, expert):
        pl.semaphore_signal(barrier, inc=1, device_id=(island, expert), device_id_type=MESH)

    loop(1, 32, lambda i: tell(isl, lax.rem(t + i, 32)))
    for d in range(1, 4):
        for k in range(2):
            tell(yh * 4 + lax.rem(x + d, 4), base + 2 * c + k)
        tell(lax.rem(yh + d, 4) * 4 + x, base + 2 * place_at[d] + core)
        tell(lax.rem(yh + d, 4) * 4 + x, t)

    @pl.when(away)
    def _():
        for q in range(4):
            tell(yh_cols * 4 + x, base + 2 * q + core)

    for load in loads[:2]:
        load.wait()

    row = lax.broadcasted_iota(jnp.int32, (chunk, cw), 0)
    col = lax.broadcasted_iota(jnp.int32, (chunk, cw), 1)
    put0 = (col == row).astype(F32).astype(BF16)
    put1 = (col == row + chunk).astype(F32).astype(BF16)

    def dot(a, b):
        return jnp.dot(a, b, preferred_element_type=F32)

    tile = (dot(gate_ref[...], put0) + dot(up_ref[...], put1)).astype(BF16)
    gut[0] = tile[:half]
    gut[1] = tile[half:]
    pl.semaphore_wait(barrier, jnp.where(away, 47, 43))

    def first_stage(tile, at, s):
        for d in (0, 1, 3, 2):
            expert = base + 2 * place_at[d] + core
            dst, r = at
            if d:
                send(tile, dst, s, r, lax.rem(yh + d, 4) * 4 + x, expert)
            else:

                @pl.when(away)
                def _():
                    send(tile, dst, s, r, isl, expert)

                @pl.when(jnp.logical_not(away))
                def _():
                    pltpu.make_async_copy(tile, dst, r).start()

    for h in range(2):
        first_stage(gut.at[h], (gu.at[0, c, h], gu_r.at[0, c, h]), gus1_s)
    for load in loads[2:5]:
        load.wait()
    down = down_ref[...].astype(BF16)
    dt[...] = (dot(down[:half], put0) + dot(down[half:], put1)).astype(BF16)

    n_tok = tok.shape[0]
    slot = lax.broadcasted_iota(jnp.int32, (4 * SLOT, n_tok), 0)
    named = lax.div(slot, SLOT)
    member = jnp.zeros((4 * SLOT, n_tok), F32)
    weight = jnp.zeros((1, n_tok), F32)
    for j in range(ids_ref.shape[0]):
        ids = ids_ref[j]
        member = member + (ids == named).astype(F32)
        weight = weight + jnp.where(ids < 4, gw_ref[j], 0.0)
    before = (
        lax.broadcasted_iota(jnp.int32, (n_tok, n_tok), 0)
        < lax.broadcasted_iota(jnp.int32, (n_tok, n_tok), 1)
    ).astype(F32).astype(BF16)
    rank = dot(member.astype(BF16), before)
    picked = jnp.where(rank == lax.rem(slot, CAP).astype(F32), member, 0.0)
    of_x = lax.rem(slot, SLOT) < CAP
    picked_x = jnp.where(of_x, picked, 0.0)
    sel[0] = picked_x.astype(BF16)
    sel[1] = jnp.where(of_x, 0.0, picked).astype(BF16)
    high = weight.astype(BF16)
    rest = weight - high.astype(F32)
    mid = rest.astype(BF16)
    low = (rest - mid.astype(F32)).astype(BF16)
    layer = lax.broadcasted_iota(jnp.int32, (8, n_tok), 0)
    three = jnp.where(layer == 0, high.astype(F32), 0.0)
    three = jnp.where(layer == 1, mid.astype(F32), three)
    three = jnp.where(layer == 2, low.astype(F32), three).astype(BF16)
    split = lax.dot_general(three, sel[0], COLS_T, preferred_element_type=F32)
    grow[...] = jnp.zeros(grow.shape, F32)
    grow[:, 0:4 * SLOT] = split[0:1] + split[1:2] + split[2:3]

    for load in loads[5:]:
        load.wait()

    def columns_of(p):
        row = lax.rem(yh + lag(lax.div(p, 2)), 4)
        return pl.ds(pl.multiple_of((2 * row + lax.rem(p, 2)) * cw, LANES), cw)

    def dispatch(p):
        cols = columns_of(p)
        sbuf[p] = (dot(sel[0], tok[:, cols]) + dot(sel[1], tgt[:, cols])).astype(BF16)
        for j in range(4):
            block = sbuf.at[p, pl.ds(j * SLOT, SLOT)]

            @pl.when(8 * j + p != t)
            def _():
                send(block, xyb.at[t], xy_s, xy_r, isl, 8 * j + p)
                send(grow, gbuf.at[t], g_s, g_r, isl, 8 * j + p)

            @pl.when(8 * j + p == t)
            def _():
                pltpu.make_async_copy(block, xyb.at[t], xy_r).start()
                pltpu.make_async_copy(grow, gbuf.at[t], g_r).start()

    loop(0, 8, dispatch)
    first_stage(dt, (dd.at[0, c], d_r.at[0, c]), ds1_s)

    def pass_on(buf, s, r, rel, to, island, *at):
        wait_for(buf.at[(rel, *at)], r.at[(rel, *at)])
        send(buf.at[(rel, *at)], buf.at[(to, *at)], s, r.at[(to, *at)], island, t)

    def around(buf, s, r, *h):
        def body(q):
            wait_for(buf.at[(0, q, *h)], r.at[(0, q, *h)])
            for to, island in ((3, right), (1, left)):
                send(buf.at[(0, q, *h)], buf.at[(to, q, *h)], s, r.at[(to, q, *h)], island, t)

        loop(0, 4, body)

    def forward(buf, s, r, *h):
        def body(q):
            pass_on(buf, s, r, 3, 2, right, q, *h)
            pass_on(buf, s, r, 1, 2, left, q + 2, *h)

        loop(0, 2, body)

    def others(buf, r, *h):
        def body(q):
            wait_for(buf.at[(3, q + 2, *h)], r.at[(3, q + 2, *h)])
            wait_for(buf.at[(1, q, *h)], r.at[(1, q, *h)])

        loop(0, 2, body)

    def far(buf, r, *h):
        loop(0, 4, lambda q: wait_for(buf.at[(2, q, *h)], r.at[(2, q, *h)]))

    def moments(i):
        here, there = columns_of(2 * near(i) + core), columns_of(2 * near(i) + 1 - core)
        for j, ref in enumerate((m_hbm, v_hbm)):
            pltpu.make_async_copy(ref.at[:, here], mv.at[i, 0, j], mv_r.at[0]).start()
            send(ref.at[:, there], mv.at[i, 1, j], mv_s, mv_r.at[1], isl, pair)

    for h in range(2):
        around(gu, gu_s, gu_r, h)
    loop(0, 4, moments)
    for h in range(2):
        forward(gu, gu_s, gu_r, h)
    around(dd, d_s, d_r)

    in_low = lax.broadcasted_iota(jnp.int32, (8 * CAP, cw), 1) < chunk

    def spread(v, h, rows):
        turned = pltpu.roll(v, chunk, 1)
        up_rows = pl.ds(rows.start + 32 * CAP, rows.size)
        lhs[2 * h, rows] = jnp.where(in_low, v, 0.0).astype(BF16)
        lhs[2 * h, up_rows] = jnp.where(in_low, 0.0, turned).astype(BF16)
        lhs[2 * h + 1, rows] = jnp.where(in_low, turned, 0.0).astype(BF16)
        lhs[2 * h + 1, up_rows] = jnp.where(in_low, 0.0, v).astype(BF16)

    wait_for(xyb, xy_r)
    wait_for(gbuf, g_r)

    is_own = lax.broadcasted_iota(jnp.int32, (8 * CAP, LANES), 1) == SLOT * e + lax.rem(
        lax.broadcasted_iota(jnp.int32, (8 * CAP, LANES), 0), CAP
    )

    def unpack(i):
        v = xyb[pl.ds(8 * i, 8)].astype(F32)
        rows = pl.ds(pl.multiple_of(i * 8 * CAP, 8 * CAP), 8 * CAP)
        xv = v[:, :CAP].reshape(8 * CAP, cw)
        xs[rows] = xv.astype(BF16)
        ys[i] = v[:, CAP:].reshape(8 * CAP, cw)
        every = jnp.broadcast_to(gbuf[pl.ds(8 * i, 8)], (8, CAP, LANES)).reshape(8 * CAP, LANES)
        total = jnp.sum(jnp.where(is_own, every, 0.0), axis=1, keepdims=True)
        gs[i] = jnp.broadcast_to(total, (8 * CAP, LANES))
        spread(xv, core, rows)

    loop(0, 4, unpack)
    send(xs, xp, xp_s, xp_r, isl, pair)
    wait_for(xp, xp_r)

    def unpack_pair(i):
        rows = pl.ds(pl.multiple_of(i * 8 * CAP, 8 * CAP), 8 * CAP)
        spread(xp[rows].astype(F32), 1 - core, rows)

    loop(0, 4, unpack_pair)

    def pre(rel):
        made = lax.dot_general(
            lhs[lax.rem(x + rel, 4)], gu[rel].reshape(4 * hid, cw), COLS_T, preferred_element_type=F32
        )
        return made.reshape(2, 4, 8 * CAP, 4 * hid)

    part[...] = pre(0)
    for h in range(2):
        others(gu, gu_r, h)
    part[...] += pre(1)
    part[...] += pre(3)
    for h in range(2):
        far(gu, gu_r, h)
    part[...] += pre(2)
    pb[...] = part[...].astype(BF16)
    part_rows = 4 * CAP
    for h in range(2):
        rows = pl.ds(h * part_rows, part_rows)
        for d in range(1, 4):
            q = lax.rem(c + d, 4)
            to = base + 2 * q + core
            send(pb.at[:, q, rows], pr.at[4 - d, :, rows], p_s, p_r.at[4 - d, h], isl, to)
    forward(dd, d_s, d_r)
    mine = 4 * core + c

    def activate(h):
        rows = pl.ds(h * part_rows, part_rows)
        for d in range(1, 4):
            wait_for(pr.at[d, :, rows], p_r.at[d, h])
        gate_sum, up_sum = (
            part[j, c, rows] + pr[1, j, rows].astype(F32) + pr[2, j, rows].astype(F32) + pr[3, j, rows].astype(F32)
            for j in range(2)
        )
        ab[mine, rows] = (gate_sum * jax.nn.sigmoid(gate_sum) * up_sum).astype(BF16)
        block = ab.at[mine, rows]
        loop(1, 8, lambda i: send(block, block, a_s, a_r.at[h], isl, base + lax.rem(pos + i, 8)))

    for h in range(2):
        activate(h)

    others(dd, d_r)
    far(dd, d_r)
    for j in range(2):
        rel = lax.rem(2 * (1 - core) + j + 4 - x, 4)
        send(dd.at[rel], dx.at[j], dx_s, dx_r.at[j], isl, pair)
    in_low_h = lax.broadcasted_iota(jnp.int32, (half, cw), 1) < chunk

    def lay(k, q, w0, w1):
        top = pl.multiple_of(q * hid, hid)
        w0, w1 = w0.astype(F32), w1.astype(F32)
        wn[k, pl.ds(top, half)] = jnp.where(in_low_h, w0, pltpu.roll(w1, chunk, 1)).astype(BF16)
        wn[k, pl.ds(top + half, half)] = jnp.where(in_low_h, pltpu.roll(w0, chunk, 1), w1).astype(BF16)

    rel0 = lax.rem(2 * core + 4 - x, 4)
    rel1 = lax.rem(2 * core + 5 - x, 4)
    loop(0, 4, lambda q: lay(core, q, dd[rel0, q], dd[rel1, q]))
    for j in range(2):
        wait_for(dx.at[j], dx_r.at[j])
    loop(0, 4, lambda q: lay(1 - core, q, dx[0, q], dx[1, q]))

    half_rows = 4 * part_rows
    unit = lax.broadcasted_iota(jnp.int32, (4 * hid, 2 * hid), 0)
    place = lax.broadcasted_iota(jnp.int32, (4 * hid, 2 * hid), 1)
    of_core = lax.div(place, hid)
    want = c * hid + lax.rem(place, hid)
    takes = [jnp.logical_and(unit == want, of_core == k).astype(F32).astype(BF16) for k in range(2)]

    for h in range(2):
        some = slice(h * part_rows, (h + 1) * part_rows)
        rows = pl.ds(h * half_rows, half_rows)
        wait_for(ab.at[pl.ds(0, 7), pl.ds(0, part_rows)], a_r.at[h])
        acts = [ab[4 * k:4 * k + 4, some].reshape(half_rows, 4 * hid) for k in range(2)]
        g = gs[:, some, 0:1].reshape(half_rows, 1)
        output = dot(acts[0], wn[0]) + dot(acts[1], wn[1])
        eb[0, rows] = (g * (g * output - ys[:, some].reshape(half_rows, cw))).astype(BF16)
        for i, (dz, dy) in ((1, (1, 0)), (2, (0, 1)), (3, (1, 1))):
            expert = base + 2 * beside(dz, dy) + core
            send(eb.at[0, rows], eb.at[i, rows], e_s, e_r.at[i], isl, expert)
        own[rows] = (dot(acts[0], takes[0]) + dot(acts[1], takes[1])).astype(BF16)

    for j in range(2):
        wait_for(mv.at[pl.ds(0, 2)], mv_r.at[j])

    def step_of(i):
        @pl.when(i > 0)
        def _():
            wait_for(eb.at[i], e_r.at[i])

        gr[...] = lax.dot_general(own[...], eb[i], ROWS_T, preferred_element_type=F32)
        for k in range(2):
            grad = gr[k * hid:(k + 1) * hid]
            side = flip(core, k)
            first = beta_first * mv[i, side, 0].astype(F32) + (1.0 - beta_first) * grad
            second = beta_second * mv[i, side, 1].astype(F32) + (1.0 - beta_second) * grad * grad
            step = first / (jnp.sqrt(second) + epsilon)
            upper, lower = step[:half], step[half:]
            ub[i, k, 0] = jnp.where(in_low_h, upper, pltpu.roll(lower, chunk, 1)).astype(BF16)
            ub[i, k, 1] = jnp.where(in_low_h, pltpu.roll(upper, chunk, 1), lower).astype(BF16)
            for j in range(2):
                stays = jnp.logical_and(2 * core + j == x, core == k)
                dst, r = r1.at[x, i], u_r.at[x, i]

                @pl.when(jnp.logical_not(stays))
                def _():
                    send(ub.at[i, k, j], dst, u_s, r, yh * 4 + 2 * core + j, base + 2 * c + k)

                @pl.when(stays)
                def _():
                    pltpu.make_async_copy(ub.at[i, k, j], dst, r).start()

    def column(i):
        for j in range(4):
            wait_for(r1.at[j, i], u_r.at[j, i])
        total = r1[0, i].astype(F32) + r1[1, i].astype(F32) + r1[2, i].astype(F32) + r1[3, i].astype(F32)
        st[i] = total.astype(st.dtype)
        to = lax.rem(yh + lag(near(i)), 4)

        @pl.when(to != yh)
        def _():
            send(st.at[i], r2.at[yh], t_s, t_r.at[yh], to * 4 + x, t)

        @pl.when(to == yh)
        def _():
            pltpu.make_async_copy(st.at[i], r2.at[yh], t_r.at[yh]).start()

    def both(i):
        step_of(i)

        @pl.when(i > 0)
        def _():
            column(i - 1)

    loop(0, 4, both)
    column(jnp.int32(3))
    loop(0, 4, lambda i: wait_for(r2.at[i], t_r.at[i]))
    out_ref[...] = r2[0].astype(F32) + r2[1].astype(F32) + r2[2].astype(F32) + r2[3].astype(F32)

    for buf, s, s1 in ((gu, gu_s, gus1_s), (dd, d_s, ds1_s)):
        wait_for(buf.at[pl.ds(0, 3)], s)

        @pl.when(away)
        def _():
            wait_for(buf.at[0], s1)

        @pl.when(home)
        def _():
            wait_for(buf.at[0, pl.ds(0, 3)], s1)

    wait_for(xyb.at[pl.ds(0, 31)], xy_s)
    wait_for(gbuf.at[pl.ds(0, 31)], g_s)
    wait_for(eb.at[pl.ds(0, 3)], e_s)
    wait_for(xs, xp_s)
    wait_for(dx, dx_s)
    wait_for(mv.at[pl.ds(0, 2)], mv_s)
    wait_for(pr.at[pl.ds(0, 3)], p_s)
    wait_for(ab.at[pl.ds(0, 7)], a_s)
    keeps = core == lax.div(x, 2)

    @pl.when(keeps)
    def _():
        wait_for(r1.at[pl.ds(0, 3)], u_s)

    @pl.when(jnp.logical_not(keeps))
    def _():
        wait_for(r1, u_s)

    wait_for(st.at[pl.ds(0, 3)], t_s)


def summed_steps(tokens, targets, expert_ids, gate_weights, gate_proj, up_proj, down_global, first, second):
    n_tok, width = tokens.shape
    hid, chunk = gate_proj.shape
    half, cw = hid // 2, 2 * chunk
    rows = 32 * CAP
    dma = pltpu.SemaphoreType.DMA
    hbm = pl.BlockSpec(memory_space=pltpu.HBM)
    vmem = pl.BlockSpec(memory_space=pltpu.VMEM)
    scratch = [
        pltpu.VMEM(expert_ids.shape, jnp.int32),
        pltpu.VMEM(gate_weights.shape, F32),
        pltpu.VMEM((hid, chunk), BF16),
        pltpu.VMEM((hid, chunk), BF16),
        pltpu.VMEM((hid, chunk), F32),
        pltpu.VMEM((n_tok, width), BF16),
        pltpu.VMEM((n_tok, width), BF16),
        pltpu.VMEM((2, 4 * SLOT, n_tok), BF16),
        pltpu.VMEM((1, LANES), F32),
        pltpu.VMEM((32, 1, LANES), F32),
        pltpu.VMEM((8, 4 * SLOT, cw), BF16),
        pltpu.VMEM((32, SLOT, cw), BF16),
        pltpu.VMEM((rows, cw), BF16),
        pltpu.VMEM((rows, cw), BF16),
        pltpu.VMEM((4, 8 * CAP, cw), F32),
        pltpu.VMEM((4, 8 * CAP, LANES), F32),
        pltpu.VMEM((4, 2 * rows, cw), BF16),
        pltpu.VMEM((2, half, cw), BF16),
        pltpu.VMEM((half, cw), BF16),
        pltpu.VMEM((4, 4, 2, half, cw), BF16),
        pltpu.VMEM((4, 4, half, cw), BF16),
        pltpu.VMEM((2, 4, half, cw), BF16),
        pltpu.VMEM((4, 2, 2, hid, cw), BF16),
        pltpu.VMEM((2, 4, 8 * CAP, 4 * hid), F32),
        pltpu.VMEM((2, 4, 8 * CAP, 4 * hid), BF16),
        pltpu.VMEM((4, 2, 8 * CAP, 4 * hid), BF16),
        pltpu.VMEM((8, 8 * CAP, 4 * hid), BF16),
        pltpu.VMEM((2, 4 * hid, cw), BF16),
        pltpu.VMEM((4, rows, cw), BF16),
        pltpu.VMEM((rows, 2 * hid), BF16),
        pltpu.VMEM((2 * hid, cw), F32),
        pltpu.VMEM((4, 2, 2, half, cw), BF16),
        pltpu.VMEM((4, 4, half, cw), BF16),
        pltpu.VMEM((4, half, cw), BF16),
        pltpu.VMEM((4, half, cw), BF16),
        dma((7,)),
        dma, dma((4, 4, 2)), dma,
        dma, dma((4, 4)), dma,
        dma, dma, dma, dma, dma, dma,
        dma, dma((2,)),
        dma, dma((2,)),
        dma, dma((4, 2)),
        dma, dma((2,)),
        dma, dma((4,)),
        dma, dma((4, 4)),
        dma, dma((4,)),
    ]
    return pl.pallas_call(
        kernel,
        out_shape=jax.ShapeDtypeStruct((half, cw), F32),
        in_specs=[hbm] * 9,
        out_specs=vmem,
        scratch_shapes=scratch,
        compiler_params=pltpu.CompilerParams(
            collective_id=0, has_side_effects=True, vmem_limit_bytes=64 * 1024 * 1024
        ),
    )(tokens, targets, expert_ids, gate_weights, gate_proj, up_proj, down_global, first, second)


def on_device(
    tokens,
    targets,
    expert_ids,
    gate_weights,
    gate_proj,
    up_proj,
    down_global,
    outer_momentum,
    inner_first,
    inner_second,
):
    islands = lax.axis_size("island")
    chunk = down_global.shape[1]
    packed = summed_steps(
        tokens[0], targets[0],
        jnp.transpose(expert_ids, (2, 0, 1)), jnp.transpose(gate_weights, (2, 0, 1)),
        gate_proj, up_proj, down_global, inner_first[0], inner_second[0],
    )
    total = jnp.concatenate([packed[:, :chunk], packed[:, chunk:]], axis=0)
    mean = inner_rate * (total / islands + decay_rate * down_global)
    new_momentum = outer_mu * outer_momentum + mean
    new_down = down_global - outer_rate * (mean + outer_mu * new_momentum)
    return (new_down, new_momentum)


def solution(mesh):
    return jax.shard_map(
        on_device,
        mesh=mesh,
        in_specs=(
            P(None, ("island", "expert"), None),
            P(None, ("island", "expert"), None),
            P(None, ("island", "expert"), None),
            P(None, ("island", "expert"), None),
            P("expert", "island"),
            P("expert", "island"),
            P("expert", "island"),
            P("expert", "island"),
            P("island", "expert", None),
            P("island", "expert", None),
        ),
        out_specs=(P("expert", "island"), P("expert", "island")),
        check_vma=False,
    )
```

```python
import jax
import jax.numpy as jnp
from jax import lax
from jax.experimental import pallas as pl
from jax.experimental.pallas import tpu as pltpu
from jax.sharding import PartitionSpec as P

CAP = 8
SLOT = 2 * CAP
LANES = 128

beta_first = 0.9
beta_second = 0.95
inner_rate = 0.01
decay_rate = 0.1
epsilon = 1e-08
outer_rate = 0.7
outer_mu = 0.9

F32 = jnp.float32
BF16 = jnp.bfloat16
MESH = pl.DeviceIdType.MESH
ROWS_T = (((0,), (0,)), ((), ()))
COLS_T = (((1,), (1,)), ((), ()))


def wait_for(ref, sem):
    pltpu.make_async_copy(ref, ref, sem).wait()


def loop(low, high, body):
    lax.fori_loop(low, high, lambda i, _: (body(i), 0)[1], 0)


def kernel(
    tok_hbm, tgt_hbm, ids_hbm, gw_hbm, gate_hbm, up_hbm, down_hbm, m_hbm, v_hbm,
    out_ref,
    ids_ref, gw_ref, gate_ref, up_ref, down_ref, tok, tgt, sel, grow, gbuf, sbuf, xyb, xs, xp, ys, gs, lhs,
    gut, dt, gu, dd, dx, mv, part, pb, pr, ab, wn, eb, own, gr, ub, r1, st, r2,
    in_sem, gu_s, gu_r, gus1_s, d_s, d_r, ds1_s, xy_s, xy_r, g_s, g_r, xp_s, xp_r, dx_s, dx_r,
    mv_s, mv_r, p_s, p_r, a_s, a_r, e_s, e_r, u_s, u_r, t_s, t_r,
):
    isl = lax.axis_index("island")
    t = lax.axis_index("expert")
    x, yh = lax.rem(isl, 4), lax.div(isl, 4)
    e, pos = lax.div(t, 8), lax.rem(t, 8)
    c, core = lax.div(pos, 2), lax.rem(pos, 2)
    base = 8 * e
    pair = t + 1 - 2 * core
    right = yh * 4 + lax.rem(x + 1, 4)
    left = yh * 4 + lax.rem(x + 3, 4)
    hid, chunk = gate_ref.shape
    half = hid // 2
    cw = 2 * chunk
    odd = lax.rem(yh, 2)

    def lag(place):
        low = 3 - 2 * place
        high = jnp.where(place == 2, 2 * odd, 2 - 2 * odd)
        return jnp.where(place < 2, low, high)

    yh_cols = lax.rem(yh + lag(c), 4)
    home = yh_cols == yh
    away = yh_cols != yh
    place_at = (2 + odd, 0, 3 - odd, 1)
    zp, yl = lax.div(c, 2), lax.rem(c, 2)

    def flip(bit, by):
        return bit + by - 2 * bit * by

    def beside(dz, dy):
        return 2 * flip(zp, dz) + flip(yl, dy)

    def near(i):
        return beside(lax.rem(i, 2), lax.div(i, 2))

    def send(src, dst, s, r, island, expert):
        pltpu.make_async_remote_copy(
            src_ref=src, dst_ref=dst, send_sem=s, recv_sem=r,
            device_id=(island, expert), device_id_type=MESH,
        ).start()

    loads = [
        pltpu.make_async_copy(src, dst, in_sem.at[i])
        for i, (src, dst) in enumerate((
            (gate_hbm, gate_ref), (up_hbm, up_ref), (down_hbm, down_ref), (ids_hbm, ids_ref),
            (gw_hbm, gw_ref), (tok_hbm, tok), (tgt_hbm, tgt),
        ))
    ]
    for load in loads:
        load.start()

    barrier = pltpu.get_barrier_semaphore()

    def tell(island, expert):
        pl.semaphore_signal(barrier, inc=1, device_id=(island, expert), device_id_type=MESH)

    loop(1, 32, lambda i: tell(isl, lax.rem(t + i, 32)))
    for d in range(1, 4):
        for k in range(2):
            tell(yh * 4 + lax.rem(x + d, 4), base + 2 * c + k)
        tell(lax.rem(yh + d, 4) * 4 + x, base + 2 * place_at[d] + core)
        tell(lax.rem(yh + d, 4) * 4 + x, t)

    @pl.when(away)
    def _():
        for q in range(4):
            tell(yh_cols * 4 + x, base + 2 * q + core)

    for load in loads[:2]:
        load.wait()

    row = lax.broadcasted_iota(jnp.int32, (chunk, cw), 0)
    col = lax.broadcasted_iota(jnp.int32, (chunk, cw), 1)
    put0 = (col == row).astype(F32).astype(BF16)
    put1 = (col == row + chunk).astype(F32).astype(BF16)

    def dot(a, b):
        return jnp.dot(a, b, preferred_element_type=F32)

    tile = (dot(gate_ref[...], put0) + dot(up_ref[...], put1)).astype(BF16)
    gut[0] = tile[:half]
    gut[1] = tile[half:]
    pl.semaphore_wait(barrier, jnp.where(away, 47, 43))

    def first_stage(tile, at, s):
        for d in (0, 1, 3, 2):
            expert = base + 2 * place_at[d] + core
            dst, r = at
            if d:
                send(tile, dst, s, r, lax.rem(yh + d, 4) * 4 + x, expert)
            else:

                @pl.when(away)
                def _():
                    send(tile, dst, s, r, isl, expert)

                @pl.when(jnp.logical_not(away))
                def _():
                    pltpu.make_async_copy(tile, dst, r).start()

    for h in range(2):
        first_stage(gut.at[h], (gu.at[0, c, h], gu_r.at[0, c, h]), gus1_s)
    for load in loads[2:5]:
        load.wait()
    down = down_ref[...].astype(BF16)
    dt[...] = (dot(down[:half], put0) + dot(down[half:], put1)).astype(BF16)

    n_tok = tok.shape[0]
    slot = lax.broadcasted_iota(jnp.int32, (4 * SLOT, n_tok), 0)
    named = lax.div(slot, SLOT)
    member = jnp.zeros((4 * SLOT, n_tok), F32)
    weight = jnp.zeros((1, n_tok), F32)
    for j in range(ids_ref.shape[0]):
        ids = ids_ref[j]
        member = member + (ids == named).astype(F32)
        weight = weight + jnp.where(ids < 4, gw_ref[j], 0.0)
    before = (
        lax.broadcasted_iota(jnp.int32, (n_tok, n_tok), 0)
        < lax.broadcasted_iota(jnp.int32, (n_tok, n_tok), 1)
    ).astype(F32).astype(BF16)
    rank = dot(member.astype(BF16), before)
    picked = jnp.where(rank == lax.rem(slot, CAP).astype(F32), member, 0.0)
    of_x = lax.rem(slot, SLOT) < CAP
    picked_x = jnp.where(of_x, picked, 0.0)
    sel[0] = picked_x.astype(BF16)
    sel[1] = jnp.where(of_x, 0.0, picked).astype(BF16)
    high = weight.astype(BF16)
    rest = weight - high.astype(F32)
    mid = rest.astype(BF16)
    low = (rest - mid.astype(F32)).astype(BF16)
    layer = lax.broadcasted_iota(jnp.int32, (8, n_tok), 0)
    three = jnp.where(layer == 0, high.astype(F32), 0.0)
    three = jnp.where(layer == 1, mid.astype(F32), three)
    three = jnp.where(layer == 2, low.astype(F32), three).astype(BF16)
    split = lax.dot_general(three, sel[0], COLS_T, preferred_element_type=F32)
    grow[...] = jnp.zeros(grow.shape, F32)
    grow[:, 0:4 * SLOT] = split[0:1] + split[1:2] + split[2:3]

    for load in loads[5:]:
        load.wait()

    def columns_of(p):
        row = lax.rem(yh + lag(lax.div(p, 2)), 4)
        return pl.ds(pl.multiple_of((2 * row + lax.rem(p, 2)) * cw, LANES), cw)

    def dispatch(p):
        cols = columns_of(p)
        sbuf[p] = (dot(sel[0], tok[:, cols]) + dot(sel[1], tgt[:, cols])).astype(BF16)
        for j in range(4):
            block = sbuf.at[p, pl.ds(j * SLOT, SLOT)]

            @pl.when(8 * j + p != t)
            def _():
                send(block, xyb.at[t], xy_s, xy_r, isl, 8 * j + p)
                send(grow, gbuf.at[t], g_s, g_r, isl, 8 * j + p)

            @pl.when(8 * j + p == t)
            def _():
                pltpu.make_async_copy(block, xyb.at[t], xy_r).start()
                pltpu.make_async_copy(grow, gbuf.at[t], g_r).start()

    loop(0, 8, dispatch)
    first_stage(dt, (dd.at[0, c], d_r.at[0, c]), ds1_s)

    def pass_on(buf, s, r, rel, to, island, *at):
        wait_for(buf.at[(rel, *at)], r.at[(rel, *at)])
        send(buf.at[(rel, *at)], buf.at[(to, *at)], s, r.at[(to, *at)], island, t)

    def around(buf, s, r, *h):
        def body(q):
            wait_for(buf.at[(0, q, *h)], r.at[(0, q, *h)])
            for to, island in ((3, right), (1, left)):
                send(buf.at[(0, q, *h)], buf.at[(to, q, *h)], s, r.at[(to, q, *h)], island, t)

        loop(0, 4, body)

    def forward(buf, s, r, *h):
        def body(q):
            pass_on(buf, s, r, 3, 2, right, q, *h)
            pass_on(buf, s, r, 1, 2, left, q + 2, *h)

        loop(0, 2, body)

    def others(buf, r, *h):
        def body(q):
            wait_for(buf.at[(3, q + 2, *h)], r.at[(3, q + 2, *h)])
            wait_for(buf.at[(1, q, *h)], r.at[(1, q, *h)])

        loop(0, 2, body)

    def far(buf, r, *h):
        loop(0, 4, lambda q: wait_for(buf.at[(2, q, *h)], r.at[(2, q, *h)]))

    def moments(i):
        here, there = columns_of(2 * near(i) + core), columns_of(2 * near(i) + 1 - core)
        for j, ref in enumerate((m_hbm, v_hbm)):
            pltpu.make_async_copy(ref.at[:, here], mv.at[i, 0, j], mv_r.at[0]).start()
            send(ref.at[:, there], mv.at[i, 1, j], mv_s, mv_r.at[1], isl, pair)

    for h in range(2):
        around(gu, gu_s, gu_r, h)
    loop(0, 4, moments)
    for h in range(2):
        forward(gu, gu_s, gu_r, h)
    around(dd, d_s, d_r)

    in_low = lax.broadcasted_iota(jnp.int32, (8 * CAP, cw), 1) < chunk

    def spread(v, h, rows):
        turned = pltpu.roll(v, chunk, 1)
        up_rows = pl.ds(rows.start + 32 * CAP, rows.size)
        lhs[2 * h, rows] = jnp.where(in_low, v, 0.0).astype(BF16)
        lhs[2 * h, up_rows] = jnp.where(in_low, 0.0, turned).astype(BF16)
        lhs[2 * h + 1, rows] = jnp.where(in_low, turned, 0.0).astype(BF16)
        lhs[2 * h + 1, up_rows] = jnp.where(in_low, 0.0, v).astype(BF16)

    wait_for(xyb, xy_r)
    wait_for(gbuf, g_r)

    is_own = lax.broadcasted_iota(jnp.int32, (8 * CAP, LANES), 1) == SLOT * e + lax.rem(
        lax.broadcasted_iota(jnp.int32, (8 * CAP, LANES), 0), CAP
    )

    def unpack(i):
        v = xyb[pl.ds(8 * i, 8)].astype(F32)
        rows = pl.ds(pl.multiple_of(i * 8 * CAP, 8 * CAP), 8 * CAP)
        xv = v[:, :CAP].reshape(8 * CAP, cw)
        xs[rows] = xv.astype(BF16)
        ys[i] = v[:, CAP:].reshape(8 * CAP, cw)
        every = jnp.broadcast_to(gbuf[pl.ds(8 * i, 8)], (8, CAP, LANES)).reshape(8 * CAP, LANES)
        total = jnp.sum(jnp.where(is_own, every, 0.0), axis=1, keepdims=True)
        gs[i] = jnp.broadcast_to(total, (8 * CAP, LANES))
        spread(xv, core, rows)

    loop(0, 4, unpack)
    send(xs, xp, xp_s, xp_r, isl, pair)
    wait_for(xp, xp_r)

    def unpack_pair(i):
        rows = pl.ds(pl.multiple_of(i * 8 * CAP, 8 * CAP), 8 * CAP)
        spread(xp[rows].astype(F32), 1 - core, rows)

    loop(0, 4, unpack_pair)

    def pre(rel):
        made = lax.dot_general(
            lhs[lax.rem(x + rel, 4)], gu[rel].reshape(4 * hid, cw), COLS_T, preferred_element_type=F32
        )
        return made.reshape(2, 4, 8 * CAP, 4 * hid)

    part[...] = pre(0)
    for h in range(2):
        others(gu, gu_r, h)
    part[...] += pre(1)
    part[...] += pre(3)
    for h in range(2):
        far(gu, gu_r, h)
    part[...] += pre(2)
    pb[...] = part[...].astype(BF16)
    part_rows = 4 * CAP
    for h in range(2):
        rows = pl.ds(h * part_rows, part_rows)
        for d in range(1, 4):
            q = lax.rem(c + d, 4)
            to = base + 2 * q + core
            send(pb.at[:, q, rows], pr.at[4 - d, :, rows], p_s, p_r.at[4 - d, h], isl, to)
    forward(dd, d_s, d_r)
    mine = 4 * core + c

    def activate(h):
        rows = pl.ds(h * part_rows, part_rows)
        for d in range(1, 4):
            wait_for(pr.at[d, :, rows], p_r.at[d, h])
        gate_sum, up_sum = (
            part[j, c, rows] + pr[1, j, rows].astype(F32) + pr[2, j, rows].astype(F32) + pr[3, j, rows].astype(F32)
            for j in range(2)
        )
        ab[mine, rows] = (gate_sum * jax.nn.sigmoid(gate_sum) * up_sum).astype(BF16)
        block = ab.at[mine, rows]
        loop(1, 8, lambda i: send(block, block, a_s, a_r.at[h], isl, base + lax.rem(pos + i, 8)))

    for h in range(2):
        activate(h)

    others(dd, d_r)
    far(dd, d_r)
    for j in range(2):
        rel = lax.rem(2 * (1 - core) + j + 4 - x, 4)
        send(dd.at[rel], dx.at[j], dx_s, dx_r.at[j], isl, pair)
    in_low_h = lax.broadcasted_iota(jnp.int32, (half, cw), 1) < chunk

    def lay(k, q, w0, w1):
        top = pl.multiple_of(q * hid, hid)
        w0, w1 = w0.astype(F32), w1.astype(F32)
        wn[k, pl.ds(top, half)] = jnp.where(in_low_h, w0, pltpu.roll(w1, chunk, 1)).astype(BF16)
        wn[k, pl.ds(top + half, half)] = jnp.where(in_low_h, pltpu.roll(w0, chunk, 1), w1).astype(BF16)

    rel0 = lax.rem(2 * core + 4 - x, 4)
    rel1 = lax.rem(2 * core + 5 - x, 4)
    loop(0, 4, lambda q: lay(core, q, dd[rel0, q], dd[rel1, q]))
    for j in range(2):
        wait_for(dx.at[j], dx_r.at[j])
    loop(0, 4, lambda q: lay(1 - core, q, dx[0, q], dx[1, q]))

    half_rows = 4 * part_rows
    unit = lax.broadcasted_iota(jnp.int32, (4 * hid, 2 * hid), 0)
    place = lax.broadcasted_iota(jnp.int32, (4 * hid, 2 * hid), 1)
    of_core = lax.div(place, hid)
    want = c * hid + lax.rem(place, hid)
    takes = [jnp.logical_and(unit == want, of_core == k).astype(F32).astype(BF16) for k in range(2)]

    for h in range(2):
        some = slice(h * part_rows, (h + 1) * part_rows)
        rows = pl.ds(h * half_rows, half_rows)
        wait_for(ab.at[pl.ds(0, 7), pl.ds(0, part_rows)], a_r.at[h])
        acts = [ab[4 * k:4 * k + 4, some].reshape(half_rows, 4 * hid) for k in range(2)]
        g = gs[:, some, 0:1].reshape(half_rows, 1)
        output = dot(acts[0], wn[0]) + dot(acts[1], wn[1])
        eb[0, rows] = (g * (g * output - ys[:, some].reshape(half_rows, cw))).astype(BF16)
        for i, (dz, dy) in ((1, (1, 0)), (2, (0, 1)), (3, (1, 1))):
            expert = base + 2 * beside(dz, dy) + core
            send(eb.at[0, rows], eb.at[i, rows], e_s, e_r.at[i], isl, expert)
        own[rows] = (dot(acts[0], takes[0]) + dot(acts[1], takes[1])).astype(BF16)

    for j in range(2):
        wait_for(mv.at[pl.ds(0, 2)], mv_r.at[j])

    def step_of(i):
        @pl.when(i > 0)
        def _():
            wait_for(eb.at[i], e_r.at[i])

        gr[...] = lax.dot_general(own[...], eb[i], ROWS_T, preferred_element_type=F32)
        for k in range(2):
            grad = gr[k * hid:(k + 1) * hid]
            side = flip(core, k)
            first = beta_first * mv[i, side, 0].astype(F32) + (1.0 - beta_first) * grad
            second = beta_second * mv[i, side, 1].astype(F32) + (1.0 - beta_second) * grad * grad
            step = first / (jnp.sqrt(second) + epsilon)
            upper, lower = step[:half], step[half:]
            ub[i, k, 0] = jnp.where(in_low_h, upper, pltpu.roll(lower, chunk, 1)).astype(BF16)
            ub[i, k, 1] = jnp.where(in_low_h, pltpu.roll(upper, chunk, 1), lower).astype(BF16)
            for j in range(2):
                stays = jnp.logical_and(2 * core + j == x, core == k)
                dst, r = r1.at[x, i], u_r.at[x, i]

                @pl.when(jnp.logical_not(stays))
                def _():
                    send(ub.at[i, k, j], dst, u_s, r, yh * 4 + 2 * core + j, base + 2 * c + k)

                @pl.when(stays)
                def _():
                    pltpu.make_async_copy(ub.at[i, k, j], dst, r).start()

    def column(i):
        for j in range(4):
            wait_for(r1.at[j, i], u_r.at[j, i])
        total = r1[0, i].astype(F32) + r1[1, i].astype(F32) + r1[2, i].astype(F32) + r1[3, i].astype(F32)
        st[i] = total.astype(st.dtype)
        to = lax.rem(yh + lag(near(i)), 4)

        @pl.when(to != yh)
        def _():
            send(st.at[i], r2.at[yh], t_s, t_r.at[yh], to * 4 + x, t)

        @pl.when(to == yh)
        def _():
            pltpu.make_async_copy(st.at[i], r2.at[yh], t_r.at[yh]).start()

    def both(i):
        step_of(i)

        @pl.when(i > 0)
        def _():
            column(i - 1)

    loop(0, 4, both)
    column(jnp.int32(3))
    loop(0, 4, lambda i: wait_for(r2.at[i], t_r.at[i]))
    total = r2[0].astype(F32) + r2[1].astype(F32) + r2[2].astype(F32) + r2[3].astype(F32)
    out_ref[0:half] = total[:, :chunk]
    out_ref[half:hid] = pltpu.roll(total, chunk, 1)[:, :chunk]

    for buf, s, s1 in ((gu, gu_s, gus1_s), (dd, d_s, ds1_s)):
        wait_for(buf.at[pl.ds(0, 3)], s)

        @pl.when(away)
        def _():
            wait_for(buf.at[0], s1)

        @pl.when(home)
        def _():
            wait_for(buf.at[0, pl.ds(0, 3)], s1)

    wait_for(xyb.at[pl.ds(0, 31)], xy_s)
    wait_for(gbuf.at[pl.ds(0, 31)], g_s)
    wait_for(eb.at[pl.ds(0, 3)], e_s)
    wait_for(xs, xp_s)
    wait_for(dx, dx_s)
    wait_for(mv.at[pl.ds(0, 2)], mv_s)
    wait_for(pr.at[pl.ds(0, 3)], p_s)
    wait_for(ab.at[pl.ds(0, 7)], a_s)
    keeps = core == lax.div(x, 2)

    @pl.when(keeps)
    def _():
        wait_for(r1.at[pl.ds(0, 3)], u_s)

    @pl.when(jnp.logical_not(keeps))
    def _():
        wait_for(r1, u_s)

    wait_for(st.at[pl.ds(0, 3)], t_s)


def summed_steps(tokens, targets, expert_ids, gate_weights, gate_proj, up_proj, down_global, first, second):
    n_tok, width = tokens.shape
    hid, chunk = gate_proj.shape
    half, cw = hid // 2, 2 * chunk
    rows = 32 * CAP
    dma = pltpu.SemaphoreType.DMA
    hbm = pl.BlockSpec(memory_space=pltpu.HBM)
    vmem = pl.BlockSpec(memory_space=pltpu.VMEM)
    scratch = [
        pltpu.VMEM(expert_ids.shape, jnp.int32),
        pltpu.VMEM(gate_weights.shape, F32),
        pltpu.VMEM((hid, chunk), BF16),
        pltpu.VMEM((hid, chunk), BF16),
        pltpu.VMEM((hid, chunk), F32),
        pltpu.VMEM((n_tok, width), BF16),
        pltpu.VMEM((n_tok, width), BF16),
        pltpu.VMEM((2, 4 * SLOT, n_tok), BF16),
        pltpu.VMEM((1, LANES), F32),
        pltpu.VMEM((32, 1, LANES), F32),
        pltpu.VMEM((8, 4 * SLOT, cw), BF16),
        pltpu.VMEM((32, SLOT, cw), BF16),
        pltpu.VMEM((rows, cw), BF16),
        pltpu.VMEM((rows, cw), BF16),
        pltpu.VMEM((4, 8 * CAP, cw), F32),
        pltpu.VMEM((4, 8 * CAP, LANES), F32),
        pltpu.VMEM((4, 2 * rows, cw), BF16),
        pltpu.VMEM((2, half, cw), BF16),
        pltpu.VMEM((half, cw), BF16),
        pltpu.VMEM((4, 4, 2, half, cw), BF16),
        pltpu.VMEM((4, 4, half, cw), BF16),
        pltpu.VMEM((2, 4, half, cw), BF16),
        pltpu.VMEM((4, 2, 2, hid, cw), BF16),
        pltpu.VMEM((2, 4, 8 * CAP, 4 * hid), F32),
        pltpu.VMEM((2, 4, 8 * CAP, 4 * hid), BF16),
        pltpu.VMEM((4, 2, 8 * CAP, 4 * hid), BF16),
        pltpu.VMEM((8, 8 * CAP, 4 * hid), BF16),
        pltpu.VMEM((2, 4 * hid, cw), BF16),
        pltpu.VMEM((4, rows, cw), BF16),
        pltpu.VMEM((rows, 2 * hid), BF16),
        pltpu.VMEM((2 * hid, cw), F32),
        pltpu.VMEM((4, 2, 2, half, cw), BF16),
        pltpu.VMEM((4, 4, half, cw), BF16),
        pltpu.VMEM((4, half, cw), BF16),
        pltpu.VMEM((4, half, cw), BF16),
        dma((7,)),
        dma, dma((4, 4, 2)), dma,
        dma, dma((4, 4)), dma,
        dma, dma, dma, dma, dma, dma,
        dma, dma((2,)),
        dma, dma((2,)),
        dma, dma((4, 2)),
        dma, dma((2,)),
        dma, dma((4,)),
        dma, dma((4, 4)),
        dma, dma((4,)),
    ]
    return pl.pallas_call(
        kernel,
        out_shape=jax.ShapeDtypeStruct((hid, chunk), F32),
        in_specs=[hbm] * 9,
        out_specs=vmem,
        scratch_shapes=scratch,
        compiler_params=pltpu.CompilerParams(
            collective_id=0, has_side_effects=True, vmem_limit_bytes=64 * 1024 * 1024
        ),
    )(tokens, targets, expert_ids, gate_weights, gate_proj, up_proj, down_global, first, second)


def on_device(
    tokens,
    targets,
    expert_ids,
    gate_weights,
    gate_proj,
    up_proj,
    down_global,
    outer_momentum,
    inner_first,
    inner_second,
):
    islands = lax.axis_size("island")
    total = summed_steps(
        tokens[0], targets[0],
        jnp.transpose(expert_ids, (2, 0, 1)), jnp.transpose(gate_weights, (2, 0, 1)),
        gate_proj, up_proj, down_global, inner_first[0], inner_second[0],
    )
    mean = inner_rate * (total / islands + decay_rate * down_global)
    new_momentum = outer_mu * outer_momentum + mean
    new_down = down_global - outer_rate * (mean + outer_mu * new_momentum)
    return (new_down, new_momentum)


def solution(mesh):
    return jax.shard_map(
        on_device,
        mesh=mesh,
        in_specs=(
            P(None, ("island", "expert"), None),
            P(None, ("island", "expert"), None),
            P(None, ("island", "expert"), None),
            P(None, ("island", "expert"), None),
            P("expert", "island"),
            P("expert", "island"),
            P("expert", "island"),
            P("expert", "island"),
            P("island", "expert", None),
            P("island", "expert", None),
        ),
        out_specs=(P("expert", "island"), P("expert", "island")),
        check_vma=False,
    )
```
